128 devices in a mesh: ctx: 8 (over x, core), tp: 16 (over y, z).
Axes of the slice: x: 4, y: 4, z: 4, core: 2. Of those that a mesh axis runs over, the one named last changes fastest.
Arguments:
- features_in: bfloat16 [1024, 8192], P('ctx', 'tp'), may hold values from -6 to 6
- w_featurizer: bfloat16 [16, 512, 3, 8192], P(None, 'ctx', None, 'tp'), may hold values from -0.0625 to 0.0625
- filter_taps: bfloat16 [16, 512, 1024], P('tp', 'ctx'), may hold values from -0.1875 to 0.1875
- query_proj: bfloat16 [1024, 8192], P('ctx', 'tp'), may hold values from -6 to 6
- key_proj: bfloat16 [1024, 8192], P('ctx', 'tp'), may hold values from -6 to 6
- value_proj: bfloat16 [1024, 8192], P('ctx', 'tp'), may hold values from -6 to 6
- grad_mixed: bfloat16 [1024, 8192], P('ctx', 'tp'), may hold values from -1.1953125 to 1.1953125
Outputs:
- grad_features: bfloat16 [1024, 8192], P('ctx', 'tp')
- grad_featurizer: bfloat16 [16, 512, 3, 8192], P(None, 'ctx', None, 'tp')
- grad_taps: bfloat16 [16, 512, 1024], P('tp', 'ctx')
The draws below stay inside these ranges and needn't reach their ends.
All inputs are finite; a program needn't handle non-finite values.
Results may differ from the reference program's by a relative error of at most 0.018.
Values may be sent and summed in bfloat16 or wider, within the bound.
No kernel may reach another device: no remote copies, remote signals or barrier semaphores. Data moves between devices by JAX's collectives and lax.ppermute only.
A program may use at most 64 MiB of HBM per device.

```python
import jax
import jax.numpy as jnp
from jax import lax

D = 8192
L = 1024
TP_CH = 512
N_TP = 16


def steps_of(rng, dims, cuts, smallest, high):
    loudness = 1.0
    for axis_at, shards_of in cuts:
        heights = jax.random.uniform(jax.random.fold_in(jax.random.fold_in(rng, 6), axis_at), (shards_of,), jnp.float32, smallest / len(cuts), high / len(cuts))
        loudness = loudness * jnp.repeat(jnp.exp(heights), dims[axis_at] // shards_of).reshape((-1,) + (1,) * (len(dims) - 1 - axis_at))
    return loudness


def centred(own_key, extent, scale, most, cuts=(), held_as=jnp.bfloat16):
    array = scale * jax.random.normal(own_key, extent, jnp.float32)
    if cuts:
        array = array * steps_of(own_key, extent, cuts, -0.22, 0.18)
    return jnp.clip(array, -most, most).astype(held_as)


def setup_inputs(seed: int = 0) -> dict:
    streams_of = jax.random.split(jax.random.key(seed), 8)
    return {
        "features_in": centred(streams_of[0], (L, D), 1.0, 6.0, ((0, 8), (1, 16))),
        "w_featurizer": centred(streams_of[1], (D // TP_CH, TP_CH, 3, D), D ** -0.5, 0.0625, ((1, 8), (3, 16))),
        "filter_taps": centred(streams_of[2], (D // TP_CH, TP_CH, L), L ** -0.5, 0.1875, ((0, 16), (1, 8))),
        "query_proj": centred(streams_of[3], (L, D), 1.0, 6.0, ((0, 8), (1, 16))),
        "key_proj": centred(streams_of[4], (L, D), 1.0, 6.0, ((0, 8), (1, 16))),
        "value_proj": centred(streams_of[5], (L, D), 1.0, 6.0, ((0, 8), (1, 16))),
        "grad_mixed": centred(streams_of[6], (L, D), 0.15, 1.1953125, ((0, 8), (1, 16))),
    }


def reference(features_in, w_featurizer, filter_taps, query_proj, key_proj, value_proj, grad_mixed):
    seq_len = features_in.shape[0]
    width = features_in.shape[1]
    size_fft = 2 * seq_len
    weights = w_featurizer.reshape(width, 3, width)
    taps = filter_taps.reshape(width, seq_len).astype(jnp.float32)
    query = query_proj.T.astype(jnp.float32)
    keys = key_proj.T.astype(jnp.float32)
    values = value_proj.T.astype(jnp.float32)
    upstream = grad_mixed.T.astype(jnp.float32)
    product = (keys * values).astype(jnp.bfloat16)
    spec_prod = jnp.fft.rfft(product.astype(jnp.float32), size_fft, axis=-1)
    spec_taps = jnp.fft.rfft(taps, size_fft, axis=-1)
    conv_out = jnp.fft.irfft(spec_prod * spec_taps, size_fft, axis=-1)[:, :seq_len]
    grad_query = (upstream * conv_out).astype(jnp.bfloat16)
    grad_conv = (upstream * query).astype(jnp.bfloat16)
    spec_grad = jnp.fft.rfft(grad_conv.astype(jnp.float32), size_fft, axis=-1)
    grad_prod = jnp.fft.irfft(spec_grad * jnp.conj(spec_taps), size_fft, axis=-1)[:, :seq_len]
    grad_taps = jnp.fft.irfft(spec_grad * jnp.conj(spec_prod), size_fft, axis=-1)[:, :seq_len]
    grad_taps = grad_taps.astype(jnp.bfloat16).reshape(filter_taps.shape)
    grad_key = (grad_prod * values).astype(jnp.bfloat16)
    grad_value = (grad_prod * keys).astype(jnp.bfloat16)
    stacked = jnp.stack([grad_query, grad_key, grad_value], axis=0)
    grad_w = jnp.stack([jnp.dot(features_in.T, stacked[branch].T, preferred_element_type=jnp.float32).astype(jnp.bfloat16) for branch in range(3)], axis=1)
    grad_w = grad_w.reshape(w_featurizer.shape)
    block_ch = width // N_TP

    def add_block(blk, total):
        grads = lax.dynamic_slice_in_dim(stacked, blk * block_ch, block_ch, 1)
        wblock = lax.dynamic_slice_in_dim(weights, blk * block_ch, block_ch, 2)
        lhs = grads.reshape(3 * block_ch, seq_len).T
        rhs = wblock.transpose(1, 2, 0).reshape(3 * block_ch, width)
        part = jnp.dot(lhs, rhs, preferred_element_type=jnp.float32).astype(jnp.bfloat16)
        part = lax.optimization_barrier(part)
        return total + part.astype(jnp.float32)

    total = lax.fori_loop(0, N_TP, add_block, jnp.zeros((seq_len, width), jnp.float32))
    return total.astype(jnp.bfloat16), grad_w, grad_taps
```

```python
import math

import jax
import jax.numpy as jnp
import numpy as np
from jax import lax
from jax.experimental import pallas as pl
from jax.experimental.pallas import tpu as pltpu
from jax.sharding import PartitionSpec as P

BF16 = jnp.bfloat16
F32 = jnp.float32


def tables(n):
    idx = np.arange(n, dtype=np.int64)
    angle = (np.outer(idx, idx) % (2 * n)).astype(np.float64) * (math.pi / n)
    out = []
    for whole in (np.cos(angle), np.sin(angle)):
        high = whole.astype(BF16)
        out.append(high)
        out.append((whole - high.astype(np.float64)).astype(BF16))
    return out


def dot(a, b):
    return lax.dot_general(a, b, (((1,), (0,)), ((), ())), preferred_element_type=F32)


def conv_kernel(recv, taps, cos_hi, cos_lo, sin_hi, sin_lo, grads, grad_taps):
    n_src, _, chans, span = recv.shape
    n = n_src * span

    def whole(which):
        return jnp.concatenate([recv[s, which] for s in range(n_src)], axis=1)

    keys = whole(0).astype(F32)
    values = whole(1).astype(F32)
    upstream = whole(2).astype(F32)
    query = whole(3).astype(F32)
    product = (keys * values).astype(BF16)
    grad_conv = (upstream * query).astype(BF16)
    signals = jnp.concatenate([product, grad_conv, taps[...]], axis=0)
    lane = lax.broadcasted_iota(jnp.int32, (1, n), 1)
    sign = jnp.where(lane % 2 == 0, 1.0, -1.0).astype(F32)
    nyq = jnp.sum(signals.astype(F32) * sign, axis=1, keepdims=True)
    re = dot(signals, cos_hi[...]) + dot(signals, cos_lo[...])
    im = dot(signals, sin_hi[...]) + dot(signals, sin_lo[...])
    ur, gr, hr = re[:chans], re[chans : 2 * chans], re[2 * chans :]
    ui, gi, hi = im[:chans], im[chans : 2 * chans], im[2 * chans :]
    un, gn, hn = nyq[:chans], nyq[chans : 2 * chans], nyq[2 * chans :]
    weight = jnp.where(lane == 0, 0.5 / n, 1.0 / n).astype(F32)
    spec_re = jnp.concatenate([ur * hr - ui * hi, gr * hr + gi * hi, gr * ur + gi * ui], axis=0) * weight
    spec_im = jnp.concatenate([ur * hi + ui * hr, gi * hr - gr * hi, gi * ur - gr * ui], axis=0) * weight
    spec_n = jnp.concatenate([un * hn, gn * hn, gn * un], axis=0) * (0.5 / n)
    re_hi = spec_re.astype(BF16)
    re_lo = (spec_re - re_hi.astype(F32)).astype(BF16)
    im_hi = spec_im.astype(BF16)
    im_lo = (spec_im - im_hi.astype(F32)).astype(BF16)
    out = (
        dot(re_hi, cos_hi[...])
        + dot(im_hi, sin_hi[...])
        + dot(re_lo, cos_hi[...])
        + dot(im_lo, sin_hi[...])
        + dot(re_hi, cos_lo[...])
        + dot(im_hi, sin_lo[...])
        + spec_n * sign
    )
    grads[0] = (upstream * out[:chans]).astype(BF16)
    grads[1] = (out[chans : 2 * chans] * values).astype(BF16)
    grads[2] = (out[chans : 2 * chans] * keys).astype(BF16)
    grad_taps[...] = out[2 * chans :].astype(BF16)


def convolutions(recv, taps):
    n_src, _, chans, span = recv.shape
    n = n_src * span
    return pl.pallas_call(
        conv_kernel,
        out_shape=(
            jax.ShapeDtypeStruct((3, chans, n), BF16),
            jax.ShapeDtypeStruct((chans, n), BF16),
        ),
        compiler_params=pltpu.CompilerParams(vmem_limit_bytes=48 * 1024 * 1024),
        name="convolutions",
    )(recv, taps, *[jnp.asarray(t) for t in tables(n)])


def per_device(features_in, w_featurizer, filter_taps, query_proj, key_proj, value_proj, grad_mixed):
    tokens_dev, width_dev = features_in.shape
    n_ctx = lax.axis_size("ctx")
    n_tp = lax.axis_size("tp")
    sub = width_dev // n_ctx
    seq_len = tokens_dev * n_ctx
    sent = jnp.stack(
        [a.T.reshape(n_ctx, sub, tokens_dev) for a in (key_proj, value_proj, grad_mixed, query_proj)], axis=1
    )
    recv = lax.all_to_all(sent, "ctx", 0, 0)
    feats = lax.all_to_all(features_in.T.reshape(n_ctx, sub, tokens_dev), "ctx", 0, 0)
    feats = feats.transpose(1, 0, 2).reshape(sub, seq_len)
    feats = lax.all_gather(feats, "tp", axis=0, tiled=True)
    grads, grad_taps = convolutions(recv, filter_taps.reshape(sub, seq_len))
    gathered = lax.all_gather(grads, "ctx", axis=0)
    weights = (
        w_featurizer.reshape(n_tp * sub, 3, n_ctx, sub).transpose(0, 2, 1, 3).reshape(n_tp * sub, 3 * width_dev)
    )
    part = dot(weights, gathered.reshape(3 * width_dev, seq_len)).astype(BF16)
    parts = lax.all_to_all(part.reshape(n_tp, sub, seq_len), "tp", 0, 0)
    total = jnp.sum(parts.astype(F32), axis=0).astype(BF16)
    total = total.reshape(sub, n_ctx, tokens_dev).transpose(1, 0, 2)
    moved = lax.all_to_all(total, "ctx", 0, 0)
    grad_features = moved.reshape(width_dev, tokens_dev).T
    ordered = gathered.transpose(1, 0, 2, 3).reshape(3 * width_dev, seq_len)
    grad_w = lax.dot_general(feats, ordered, (((1,), (1,)), ((), ())), preferred_element_type=F32).astype(BF16)
    return grad_features, grad_w.reshape(w_featurizer.shape), grad_taps.reshape(filter_taps.shape)


def solution(mesh):
    return jax.shard_map(
        per_device,
        mesh=mesh,
        in_specs=(
            P("ctx", "tp"),
            P(None, "ctx", None, "tp"),
            P("tp", "ctx", None),
            P("ctx", "tp"),
            P("ctx", "tp"),
            P("ctx", "tp"),
            P("ctx", "tp"),
        ),
        out_specs=(P("ctx", "tp"), P(None, "ctx", None, "tp"), P("tp", "ctx", None)),
        check_vma=False,
    )
```

```python
import functools
import math

import jax
import jax.numpy as jnp
import numpy as np
from jax import lax
from jax.experimental import pallas as pl
from jax.experimental.pallas import tpu as pltpu
from jax.sharding import PartitionSpec as P

BF16 = jnp.bfloat16
F32 = jnp.float32
N_X = 4
N_CTX = 8
N_RING = 4
MIB = 1024 * 1024
ON_CHIP = pl.BlockSpec(memory_space=pltpu.VMEM)
FAR = pl.BlockSpec(memory_space=pltpu.HBM)
SCALAR = pl.BlockSpec(memory_space=pltpu.SMEM)


def vmem(mib):
    return pltpu.CompilerParams(vmem_limit_bytes=mib * MIB)


def like(*shape, dtype=BF16):
    return jax.ShapeDtypeStruct(shape, dtype)


def tables(n):
    idx = np.arange(n, dtype=np.int64)
    angle = (np.outer(idx, idx) % (2 * n)).astype(np.float64) * (math.pi / n)
    out = []
    for whole in (np.cos(angle), np.sin(angle)):
        high = whole.astype(BF16)
        out.append(high)
        out.append((whole - high.astype(np.float64)).astype(BF16))
    return [jnp.asarray(t) for t in out]


def dot(a, b):
    return lax.dot_general(a, b, (((1,), (0,)), ((), ())), preferred_element_type=F32)


def dot_t(a, b):
    return lax.dot_general(a, b, (((1,), (1,)), ((), ())), preferred_element_type=F32)


def shift_x(a, steps):
    return lax.ppermute(a, "ctx", [(i, (i + 2 * steps) % N_CTX) for i in range(N_CTX)])


def swap_core(a):
    return lax.ppermute(a, "ctx", [(i, i ^ 1) for i in range(N_CTX)])


def source(me, piece):
    back, other = piece % N_X, piece // N_X
    chip = (me // 2 + N_X - back) % N_X
    core = me % 2
    return 2 * chip + (1 - core if other else core)


def spin(a):
    pairs = [(2 * x + core, 2 * ((x + 1 - 2 * core) % N_X) + core) for x in range(N_X) for core in range(2)]
    return lax.ppermute(a, "ctx", pairs)


def gather_start(mine):
    sibling = swap_core(mine)
    return [mine, sibling, spin(mine), spin(sibling)]


def gathered_source(me, piece):
    chip, core = me // 2, me % 2
    if piece < 2:
        return 2 * chip + (core if piece == 0 else 1 - core)
    kind, theirs = (piece - 2) % 3, piece >= 5
    back = 1 - 2 * core
    if theirs:
        back, core = -back, 1 - core
    chip = (chip + N_X - (2 if kind == 2 else back)) % N_X
    return 2 * chip + (1 - core if kind == 1 else core)


def target(me, ahead, other):
    chip = (me // 2 + ahead) % N_X
    core = me % 2
    return 2 * chip + (1 - core if other else core)


def place(me, first):
    on_y, on_z = me[1] // N_RING, me[1] % N_RING
    return jnp.where((me[0] % 2 == 0) == first, on_y, on_z)


def group(me, at, k):
    return jnp.where(me[0] % 2 == 0, at * N_RING + k, k * N_RING + at)


def shift_ring(a, steps, first):
    pairs = []
    for ctx in range(N_CTX):
        for y in range(N_RING):
            for z in range(N_RING):
                along_y = (ctx % 2 == 0) == first
                to = ((y + steps) % N_RING, z) if along_y else (y, (z + steps) % N_RING)
                base = ctx * N_RING * N_RING
                pairs.append((base + y * N_RING + z, base + to[0] * N_RING + to[1]))
    return lax.ppermute(a, ("ctx", "tp"), pairs)


def part_of(index, size):
    return pl.ds(pl.multiple_of(index * size, size), size)


def prep_kernel(me, *refs):
    n_arr = len(refs) - 3 - N_X
    arrays, outs = refs[:n_arr], refs[n_arr : n_arr + N_X]
    local, turned, sems = refs[n_arr + N_X :]
    copies = [pltpu.make_async_copy(arrays[a], local.at[a], sems.at[a]) for a in range(n_arr)]
    for copy in copies:
        copy.start()
    sub = outs[0].shape[2]
    for a in range(n_arr):
        copies[a].wait()
        turned[a] = local[a].T
    for ahead in range(N_X):
        for other in range(2):
            rows = part_of(target(me[0], ahead, other), sub)
            for a in range(n_arr):
                outs[ahead][other, a] = turned[a, rows, :]


def prepare(me, arrays):
    tokens, width = arrays[0].shape
    n_arr = len(arrays)
    return pl.pallas_call(
        prep_kernel,
        out_shape=[like(2, n_arr, width // N_CTX, tokens)] * N_X,
        in_specs=[SCALAR] + [FAR] * n_arr,
        out_specs=[ON_CHIP] * N_X,
        scratch_shapes=[
            pltpu.VMEM((n_arr, tokens, width), BF16),
            pltpu.VMEM((n_arr, width, tokens), BF16),
            pltpu.SemaphoreType.DMA((n_arr,)),
        ],
        compiler_params=vmem(6),
        name="prepare",
    )(me, *[pltpu.with_memory_space_constraint(a, pltpu.HBM) for a in arrays])


def join_kernel(me, *refs):
    pieces, out = refs[:N_CTX], refs[N_CTX]
    span = pieces[0].shape[-1]
    for p in range(N_CTX):
        out[:, part_of(source(me[0], p), span)] = pieces[p][pieces[p].shape[0] - 1]


def join_features(me, pieces):
    _, sub, span = pieces[0].shape
    return pl.pallas_call(
        join_kernel,
        out_shape=like(sub, span * N_CTX),
        in_specs=[SCALAR] + [ON_CHIP] * N_CTX,
        out_specs=ON_CHIP,
        compiler_params=vmem(6),
        name="join_features",
    )(me, *pieces)


def stack_kernel(me, *refs):
    pieces, out = refs[:N_RING], refs[N_RING]
    for s in range(N_RING):
        out[pl.ds((place(me, first=False) + N_RING - s) % N_RING, 1)] = pieces[s][...][None]


def stack(me, pieces):
    return pl.pallas_call(
        stack_kernel,
        out_shape=like(N_RING, *pieces[0].shape),
        in_specs=[SCALAR] + [ON_CHIP] * N_RING,
        out_specs=ON_CHIP,
        compiler_params=vmem(6),
        name="stack_features",
    )(me, *pieces)


def signs(n):
    lane = lax.broadcasted_iota(jnp.int32, (1, n), 1)
    return jnp.where(lane % 2 == 0, 1.0, -1.0).astype(F32)


def spectrum(signals, table, n):
    nyq = jnp.sum(signals.astype(F32) * signs(n), axis=1, keepdims=True)
    re = dot(signals, table[0][...]) + dot(signals, table[1][...])
    im = dot(signals, table[2][...]) + dot(signals, table[3][...])
    return re, im, nyq


def split(a):
    high = a.astype(BF16)
    return high, (a - high.astype(F32)).astype(BF16)


def inverse(re, im, nyq, table, n):
    rows = re.shape[0]
    lane = lax.broadcasted_iota(jnp.int32, (1, n), 1)
    weight = jnp.where(lane == 0, 0.5 / n, 1.0 / n).astype(F32)
    re_hi, re_lo = split(re * weight)
    im_hi, im_lo = split(im * weight)
    both = dot(jnp.concatenate([re_hi, re_lo], axis=0), table[0][...])
    both = both + dot(jnp.concatenate([im_hi, im_lo], axis=0), table[2][...])
    low = dot(re_hi, table[1][...]) + dot(im_hi, table[3][...])
    return both[:rows] + both[rows:] + low + (nyq * (0.5 / n)) * signs(n)


def taps_kernel(*refs):
    far, taps = refs[:4], refs[4]
    table, re, im, nyq, sems = refs[5:9], refs[9], refs[10], refs[11], refs[12]
    copies = [pltpu.make_async_copy(far[i], table[i], sems.at[i]) for i in range(4)]
    for copy in copies:
        copy.start()
    for copy in copies:
        copy.wait()
    re[...], im[...], nyq[...] = spectrum(taps[...], table, taps.shape[1])


def taps_spectrum(taps):
    chans, n = taps.shape
    return pl.pallas_call(
        taps_kernel,
        out_shape=[like(n, n)] * 4 + [like(chans, n, dtype=F32)] * 2 + [like(chans, 1, dtype=F32)],
        in_specs=[FAR] * 4 + [ON_CHIP],
        out_specs=[ON_CHIP] * 7,
        scratch_shapes=[pltpu.SemaphoreType.DMA((4,))],
        compiler_params=vmem(12),
        cost_estimate=pl.CostEstimate(flops=8 * chans * n * n, bytes_accessed=8 * MIB, transcendentals=0),
        name="taps_spectrum",
    )(*[pltpu.with_memory_space_constraint(t, pltpu.HBM) for t in tables(n)], taps)


def conv_kernel(me, *refs):
    pieces = refs[:N_CTX]
    table = refs[N_CTX : N_CTX + 4]
    hr, hi, hn = refs[N_CTX + 4 : N_CTX + 7]
    grads, out_re, out_im, out_n, whole = refs[N_CTX + 7 :]
    chans, span = pieces[0].shape[-2:]
    n = N_CTX * span
    for p in range(N_CTX):
        for a in range(4):
            whole[a, :, part_of(source(me[0], p), span)] = pieces[p][a]
    product = (whole[0].astype(F32) * whole[1].astype(F32)).astype(BF16)
    grad_conv = (whole[2].astype(F32) * whole[3].astype(F32)).astype(BF16)
    re, im, nyq = spectrum(jnp.concatenate([product, grad_conv], axis=0), table, n)
    ur, gr, ui, gi, un, gn = re[:chans], re[chans:], im[:chans], im[chans:], nyq[:chans], nyq[chans:]
    hr, hi, hn = hr[...], hi[...], hn[...]
    out_re[...] = gr * ur + gi * ui
    out_im[...] = gi * ur - gr * ui
    out_n[...] = gn * un
    spec_re = jnp.concatenate([ur * hr - ui * hi, gr * hr + gi * hi], axis=0)
    spec_im = jnp.concatenate([ur * hi + ui * hr, gi * hr - gr * hi], axis=0)
    out = inverse(spec_re, spec_im, jnp.concatenate([un * hn, gn * hn], axis=0), table, n)
    grads[0] = (whole[2].astype(F32) * out[:chans]).astype(BF16)
    grads[1] = (out[chans:] * whole[1].astype(F32)).astype(BF16)
    grads[2] = (out[chans:] * whole[0].astype(F32)).astype(BF16)


def convolutions(me, pieces, table, taps_spec):
    chans, span = pieces[0].shape[-2:]
    n = N_CTX * span
    return pl.pallas_call(
        conv_kernel,
        out_shape=[like(3, chans, n)] + [like(chans, n, dtype=F32)] * 2 + [like(chans, 1, dtype=F32)],
        in_specs=[SCALAR] + [ON_CHIP] * (N_CTX + 7),
        out_specs=[ON_CHIP] * 4,
        scratch_shapes=[pltpu.VMEM((4, chans, n), BF16)],
        compiler_params=vmem(20),
        cost_estimate=pl.CostEstimate(flops=32 * chans * n * n, bytes_accessed=8 * MIB, transcendentals=0),
        name="convolutions",
    )(me, *pieces, *table, *taps_spec)


def taps_grad_kernel(*refs):
    table, (re, im, nyq), out = refs[:4], refs[4:7], refs[7]
    out[...] = inverse(re[...], im[...], nyq[...], table, out.shape[1]).astype(BF16)


def taps_grad(spec, table):
    return pl.pallas_call(
        taps_grad_kernel,
        out_shape=like(*spec[0].shape),
        in_specs=[ON_CHIP] * 7,
        out_specs=ON_CHIP,
        compiler_params=vmem(16),
        cost_estimate=pl.CostEstimate(flops=16 * MIB * 64, bytes_accessed=8 * MIB, transcendentals=0),
        name="taps_grad",
    )(*table, *spec)


def gather_pieces(mine):
    along = [mine] + [shift_x(mine, s) for s in (1, 2, 3)]
    return along + [swap_core(a) for a in along]


def assemble_kernel(which, me, *refs):
    pieces, whole = refs[: len(which)], refs[-1]
    sub = pieces[0].shape[1]
    for p, piece in zip(which, pieces, strict=True):
        for b in range(3):
            whole[part_of(b * N_CTX + gathered_source(me[0], p), sub), :] = piece[b]


def assemble(me, pieces, which):
    _, sub, n = pieces[0].shape
    return pl.pallas_call(
        functools.partial(assemble_kernel, which),
        out_shape=like(3 * N_CTX * sub, n),
        in_specs=[SCALAR] + [ON_CHIP] * len(which),
        out_specs=ON_CHIP,
        compiler_params=vmem(8),
        name="assemble",
    )(me, *pieces)


def value_kernel(steps, which, me, *refs):
    weights, held, refs = refs[0], refs[1], refs[2:]
    pieces, refs = refs[: len(which)], refs[len(which) :]
    parts = refs[: len(steps)]
    whole = held
    if which:
        whole, far_whole, sem = refs[len(steps) :]
        assemble_kernel(which, me, *pieces, whole)
        copy = pltpu.make_async_copy(whole, far_whole, sem)
        copy.start()
    for s, part in zip(steps, parts, strict=True):
        at = (place(me, first=True) + s) % N_RING
        lhs = []
        for k in range(N_RING):
            w = weights[group(me, at, k)]
            lhs.append(jnp.concatenate([w[b] for b in range(3)], axis=1))
        res = dot(jnp.concatenate(lhs, axis=0), whole[...])
        part[...] = res.astype(BF16).reshape(part.shape)
    if which:
        copy.wait()


def value_part(me, weights, whole, steps, pieces=(), which=()):
    _, _, rows, width = weights.shape
    n = whole.shape[1]
    shapes = [like(N_RING, rows, n)] * len(steps)
    specs = [ON_CHIP] * len(steps)
    if which:
        shapes += [like(*whole.shape), pltpu.HBM(whole.shape, BF16)]
        specs += [ON_CHIP, FAR]
    return pl.pallas_call(
        functools.partial(value_kernel, steps, which),
        out_shape=shapes,
        in_specs=[SCALAR] + [ON_CHIP] * (len(which) + 2),
        out_specs=specs,
        scratch_shapes=[pltpu.SemaphoreType.DMA] if which else [],
        input_output_aliases={2: len(steps)} if which else {},
        compiler_params=vmem(16),
        cost_estimate=pl.CostEstimate(
            flops=2 * len(steps) * rows * width * n, bytes_accessed=MIB // 4, transcendentals=0
        ),
        name="value_part",
    )(me, weights, whole, *pieces)


def weight_kernel(me, whole, *refs):
    feats, out, res, sems = refs[:N_RING], refs[N_RING], refs[N_RING + 1], refs[N_RING + 2]
    _, rows, n = feats[0].shape
    width = out.shape[-1]
    copies = []
    for s in range(N_RING):
        at = (place(me, first=True) + N_RING - s) % N_RING
        tall = dot_t(feats[s][...].reshape(N_RING * rows, n), whole[...]).astype(BF16)
        for k in range(N_RING):
            for b in range(3):
                res[s, k, b] = tall[k * rows : (k + 1) * rows, b * width : (b + 1) * width]
            copies.append(pltpu.make_async_copy(res.at[s, k], out.at[group(me, at, k)], sems.at[s, k]))
            copies[-1].start()
    for copy in copies:
        copy.wait()


def weight_grad(me, whole, feats):
    _, rows, n = feats[0].shape
    width = whole.shape[0] // 3
    return pl.pallas_call(
        weight_kernel,
        out_shape=pltpu.HBM((N_RING * N_RING, 3, rows, width), BF16),
        in_specs=[SCALAR] + [ON_CHIP] * (N_RING + 1),
        out_specs=FAR,
        scratch_shapes=[
            pltpu.VMEM((N_RING, N_RING, 3, rows, width), BF16),
            pltpu.SemaphoreType.DMA((N_RING, N_RING)),
        ],
        compiler_params=vmem(18),
        cost_estimate=pl.CostEstimate(flops=96 * rows * width * n, bytes_accessed=8 * MIB, transcendentals=0),
        name="weight_grad",
    )(me, whole, *feats)


def first_sum_kernel(me, *refs):
    parts, outs = refs[:N_RING], refs[N_RING:]
    for s in range(N_RING):
        k = pl.ds((place(me, first=False) + s) % N_RING, 1)
        total = parts[0][k].astype(F32)
        for i in range(1, N_RING):
            total = total + parts[i][k].astype(F32)
        outs[s][...] = total[0].astype(BF16)


def first_sum(me, parts):
    _, rows, n = parts[0].shape
    return pl.pallas_call(
        first_sum_kernel,
        out_shape=[like(rows, n)] * N_RING,
        in_specs=[SCALAR] + [ON_CHIP] * N_RING,
        out_specs=[ON_CHIP] * N_RING,
        compiler_params=vmem(6),
        name="first_sum",
    )(me, *parts)


def sum_kernel(me, *refs):
    parts, outs, whole = refs[:N_RING], refs[N_RING:-1], refs[-1]
    total = parts[0][...].astype(F32)
    for i in range(1, N_RING):
        total = total + parts[i][...].astype(F32)
    whole[...] = total.astype(BF16)
    tokens = outs[0].shape[-1]
    for ahead in range(N_X):
        for other in range(2):
            outs[ahead][other] = whole[:, part_of(target(me[0], ahead, other), tokens)]


def sum_parts(me, parts):
    rows, n = parts[0].shape
    return pl.pallas_call(
        sum_kernel,
        out_shape=[like(2, rows, n // N_CTX)] * N_X,
        in_specs=[SCALAR] + [ON_CHIP] * N_RING,
        out_specs=[ON_CHIP] * N_X,
        scratch_shapes=[pltpu.VMEM((rows, n), BF16)],
        compiler_params=vmem(6),
        name="sum_parts",
    )(me, *parts)


def finish_kernel(me, *refs):
    pieces, out, whole = refs[:N_CTX], refs[N_CTX], refs[N_CTX + 1]
    sub = pieces[0].shape[0]
    for p in range(N_CTX):
        whole[part_of(source(me[0], p), sub), :] = pieces[p][...]
    out[...] = whole[...].T


def finish(me, pieces):
    rows, tokens = pieces[0].shape
    return pl.pallas_call(
        finish_kernel,
        out_shape=like(tokens, rows * N_CTX),
        in_specs=[SCALAR] + [ON_CHIP] * N_CTX,
        scratch_shapes=[pltpu.VMEM((rows * N_CTX, tokens), BF16)],
        compiler_params=vmem(6),
        name="finish",
    )(me, *pieces)


def tie(a, b):
    return lax.optimization_barrier((a, b))


def per_device(features_in, w_featurizer, filter_taps, query_proj, key_proj, value_proj, grad_mixed):
    width_dev = features_in.shape[1]
    me = jnp.stack([lax.axis_index("ctx"), lax.axis_index("tp")]).astype(jnp.int32)
    weights = w_featurizer.transpose(0, 2, 1, 3)
    ready = prepare(me, (key_proj, value_proj, grad_mixed, query_proj, features_in))
    along = [ready[0]] + [shift_x(ready[s], s) for s in (1, 2, 3)]
    spec_taps = taps_spectrum(filter_taps.reshape(width_dev // N_CTX, -1))
    along, spec_taps = tie(along, spec_taps)
    *table, hr, hi, hn = spec_taps
    pieces = [a[0] for a in along] + [swap_core(a[1]) for a in along]
    grads, *spec = convolutions(me, pieces, table, (hr, hi, hn))
    pieces, grads = tie(pieces, grads)
    near = gather_start(grads)
    feats = join_features(me, pieces)
    feats = [feats] + [shift_ring(feats, s, first=False) for s in (1, 2, 3)]
    far, feats = tie(near[2], feats)
    last = spin(far)
    feats = stack(me, feats)
    grad_taps = taps_grad(spec, table)
    last, (grad_taps, feats) = tie(last, (grad_taps, feats))
    theirs = [swap_core(a) for a in near[2:]]
    feats = [feats] + [shift_ring(feats, s, first=True) for s in (1, 2, 3)]
    whole = assemble(me, near + theirs, (0, 1, 2, 3, 5, 6))
    part2, whole, far_whole = value_part(me, weights, whole, (2,), (last, swap_core(last)), (4, 7))
    (part1,) = value_part(me, weights, whole, (1,))
    (part3,) = value_part(me, weights, whole, (3,))
    whole, feats = tie(whole, feats)
    (part0,) = value_part(me, weights, whole, (0,))
    parts = [part0] + [shift_ring(p, s, first=True) for p, s in ((part1, 1), (part2, 2), (part3, 3))]
    parts = first_sum(me, parts)
    parts = [parts[0]] + [shift_ring(parts[s], s, first=False) for s in (1, 2, 3)]
    ready = sum_parts(me, parts)
    grad_w = weight_grad(me, far_whole, feats)
    along = [ready[0]] + [shift_x(ready[s], s) for s in (1, 2, 3)]
    along, grad_w = tie(along, grad_w)
    grad_features = finish(me, [a[0] for a in along] + [swap_core(a[1]) for a in along])
    return grad_features, grad_w.transpose(0, 2, 1, 3), grad_taps.reshape(filter_taps.shape)


def solution(mesh):
    return jax.shard_map(
        per_device,
        mesh=mesh,
        in_specs=(
            P("ctx", "tp"),
            P(None, "ctx", None, "tp"),
            P("tp", "ctx", None),
            P("ctx", "tp"),
            P("ctx", "tp"),
            P("ctx", "tp"),
            P("ctx", "tp"),
        ),
        out_specs=(P("ctx", "tp"), P(None, "ctx", None, "tp"), P("tp", "ctx", None)),
        check_vma=False,
    )
```

```python
import functools
import math

import jax
import jax.numpy as jnp
import numpy as np
from jax import lax
from jax.experimental import pallas as pl
from jax.experimental.pallas import tpu as pltpu
from jax.sharding import PartitionSpec as P

BF16 = jnp.bfloat16
F32 = jnp.float32
N_X = 4
N_CTX = 8
N_RING = 4
MIB = 1024 * 1024
ON_CHIP = pl.BlockSpec(memory_space=pltpu.VMEM)
FAR = pl.BlockSpec(memory_space=pltpu.HBM)
SCALAR = pl.BlockSpec(memory_space=pltpu.SMEM)


def vmem(mib):
    return pltpu.CompilerParams(vmem_limit_bytes=mib * MIB)


def like(*shape, dtype=BF16):
    return jax.ShapeDtypeStruct(shape, dtype)


def tables(n):
    idx = np.arange(n, dtype=np.int64)
    angle = (np.outer(idx, idx) % (2 * n)).astype(np.float64) * (math.pi / n)
    out = []
    for whole in (np.cos(angle), np.sin(angle)):
        high = whole.astype(BF16)
        out.append(high)
        out.append((whole - high.astype(np.float64)).astype(BF16))
    return [jnp.asarray(t) for t in out]


def dot(a, b):
    return lax.dot_general(a, b, (((1,), (0,)), ((), ())), preferred_element_type=F32)


def dot_t(a, b):
    return lax.dot_general(a, b, (((1,), (1,)), ((), ())), preferred_element_type=F32)


def shift_x(a, steps):
    return lax.ppermute(a, "ctx", [(i, (i + 2 * steps) % N_CTX) for i in range(N_CTX)])


def swap_core(a):
    return lax.ppermute(a, "ctx", [(i, i ^ 1) for i in range(N_CTX)])


def source(me, piece):
    back, other = piece % N_X, piece // N_X
    chip = (me // 2 + N_X - back) % N_X
    core = me % 2
    return 2 * chip + (1 - core if other else core)


def spin(a):
    pairs = [(2 * x + core, 2 * ((x + 1 - 2 * core) % N_X) + core) for x in range(N_X) for core in range(2)]
    return lax.ppermute(a, "ctx", pairs)


def gather_start(mine):
    sibling = swap_core(mine)
    return [mine, sibling, spin(mine), spin(sibling)]


def gathered_source(me, piece):
    chip, core = me // 2, me % 2
    if piece < 2:
        return 2 * chip + (core if piece == 0 else 1 - core)
    kind, theirs = (piece - 2) % 3, piece >= 5
    back = 1 - 2 * core
    if theirs:
        back, core = -back, 1 - core
    chip = (chip + N_X - (2 if kind == 2 else back)) % N_X
    return 2 * chip + (1 - core if kind == 1 else core)


def target(me, ahead, other):
    chip = (me // 2 + ahead) % N_X
    core = me % 2
    return 2 * chip + (1 - core if other else core)


def place(me, first):
    on_y, on_z = me[1] // N_RING, me[1] % N_RING
    return jnp.where((me[0] % 2 == 0) == first, on_y, on_z)


def group(me, at, k):
    return jnp.where(me[0] % 2 == 0, at * N_RING + k, k * N_RING + at)


def shift_ring(a, steps, first):
    pairs = []
    for ctx in range(N_CTX):
        for y in range(N_RING):
            for z in range(N_RING):
                along_y = (ctx % 2 == 0) == first
                to = ((y + steps) % N_RING, z) if along_y else (y, (z + steps) % N_RING)
                base = ctx * N_RING * N_RING
                pairs.append((base + y * N_RING + z, base + to[0] * N_RING + to[1]))
    return lax.ppermute(a, ("ctx", "tp"), pairs)


def part_of(index, size):
    return pl.ds(pl.multiple_of(index * size, size), size)


def prep_kernel(me, *refs):
    n_arr = len(refs) - 3 - N_X
    arrays, outs = refs[:n_arr], refs[n_arr : n_arr + N_X]
    local, turned, sems = refs[n_arr + N_X :]
    copies = [pltpu.make_async_copy(arrays[a], local.at[a], sems.at[a]) for a in range(n_arr)]
    for copy in copies:
        copy.start()
    sub = outs[0].shape[2]
    for a in range(n_arr):
        copies[a].wait()
        turned[a] = local[a].T
    for ahead in range(N_X):
        for other in range(2):
            rows = part_of(target(me[0], ahead, other), sub)
            for a in range(n_arr):
                outs[ahead][other, a] = turned[a, rows, :]


def prepare(me, arrays):
    tokens, width = arrays[0].shape
    n_arr = len(arrays)
    return pl.pallas_call(
        prep_kernel,
        out_shape=[like(2, n_arr, width // N_CTX, tokens)] * N_X,
        in_specs=[SCALAR] + [FAR] * n_arr,
        out_specs=[ON_CHIP] * N_X,
        scratch_shapes=[
            pltpu.VMEM((n_arr, tokens, width), BF16),
            pltpu.VMEM((n_arr, width, tokens), BF16),
            pltpu.SemaphoreType.DMA((n_arr,)),
        ],
        compiler_params=vmem(6),
        name="prepare",
    )(me, *[pltpu.with_memory_space_constraint(a, pltpu.HBM) for a in arrays])


def join_kernel(me, *refs):
    pieces, out = refs[:N_CTX], refs[N_CTX]
    span = pieces[0].shape[-1]
    for p in range(N_CTX):
        out[:, part_of(source(me[0], p), span)] = pieces[p][pieces[p].shape[0] - 1]


def join_features(me, pieces):
    _, sub, span = pieces[0].shape
    return pl.pallas_call(
        join_kernel,
        out_shape=like(sub, span * N_CTX),
        in_specs=[SCALAR] + [ON_CHIP] * N_CTX,
        out_specs=ON_CHIP,
        compiler_params=vmem(6),
        name="join_features",
    )(me, *pieces)


def stack_kernel(me, *refs):
    pieces, out = refs[:N_RING], refs[N_RING]
    for s in range(N_RING):
        out[pl.ds((place(me, first=False) + N_RING - s) % N_RING, 1)] = pieces[s][...][None]


def stack(me, pieces):
    return pl.pallas_call(
        stack_kernel,
        out_shape=like(N_RING, *pieces[0].shape),
        in_specs=[SCALAR] + [ON_CHIP] * N_RING,
        out_specs=ON_CHIP,
        compiler_params=vmem(6),
        name="stack_features",
    )(me, *pieces)


def signs(n):
    lane = lax.broadcasted_iota(jnp.int32, (1, n), 1)
    return jnp.where(lane % 2 == 0, 1.0, -1.0).astype(F32)


def spectrum(signals, table, n):
    nyq = jnp.sum(signals.astype(F32) * signs(n), axis=1, keepdims=True)
    re = dot(signals, table[0][...]) + dot(signals, table[1][...])
    im = dot(signals, table[2][...]) + dot(signals, table[3][...])
    return re, im, nyq


def split(a):
    high = a.astype(BF16)
    return high, (a - high.astype(F32)).astype(BF16)


def inverse(re, im, nyq, table, n):
    rows = re.shape[0]
    lane = lax.broadcasted_iota(jnp.int32, (1, n), 1)
    weight = jnp.where(lane == 0, 0.5 / n, 1.0 / n).astype(F32)
    re_hi, re_lo = split(re * weight)
    im_hi, im_lo = split(im * weight)
    both = dot(jnp.concatenate([re_hi, re_lo], axis=0), table[0][...])
    both = both + dot(jnp.concatenate([im_hi, im_lo], axis=0), table[2][...])
    low = dot(re_hi, table[1][...]) + dot(im_hi, table[3][...])
    return both[:rows] + both[rows:] + low + (nyq * (0.5 / n)) * signs(n)


def taps_kernel(*refs):
    far, taps = refs[:4], refs[4]
    table, re, im, nyq, sems = refs[5:9], refs[9], refs[10], refs[11], refs[12]
    copies = [pltpu.make_async_copy(far[i], table[i], sems.at[i]) for i in range(4)]
    for copy in copies:
        copy.start()
    for copy in copies:
        copy.wait()
    re[...], im[...], nyq[...] = spectrum(taps[...], table, taps.shape[1])


def taps_spectrum(taps):
    chans, n = taps.shape
    return pl.pallas_call(
        taps_kernel,
        out_shape=[like(n, n)] * 4 + [like(chans, n, dtype=F32)] * 2 + [like(chans, 1, dtype=F32)],
        in_specs=[FAR] * 4 + [ON_CHIP],
        out_specs=[ON_CHIP] * 7,
        scratch_shapes=[pltpu.SemaphoreType.DMA((4,))],
        compiler_params=vmem(12),
        cost_estimate=pl.CostEstimate(flops=8 * chans * n * n, bytes_accessed=8 * MIB, transcendentals=0),
        name="taps_spectrum",
    )(*[pltpu.with_memory_space_constraint(t, pltpu.HBM) for t in tables(n)], taps)


def conv_kernel(me, *refs):
    pieces = refs[:N_CTX]
    table = refs[N_CTX : N_CTX + 4]
    hr, hi, hn = refs[N_CTX + 4 : N_CTX + 7]
    grads, grad_taps, whole = refs[N_CTX + 7 :]
    chans, span = pieces[0].shape[-2:]
    n = N_CTX * span
    for p in range(N_CTX):
        for a in range(4):
            whole[a, :, part_of(source(me[0], p), span)] = pieces[p][a]
    product = (whole[0].astype(F32) * whole[1].astype(F32)).astype(BF16)
    grad_conv = (whole[2].astype(F32) * whole[3].astype(F32)).astype(BF16)
    re, im, nyq = spectrum(jnp.concatenate([product, grad_conv], axis=0), table, n)
    ur, gr, ui, gi, un, gn = re[:chans], re[chans:], im[:chans], im[chans:], nyq[:chans], nyq[chans:]
    hr, hi, hn = hr[...], hi[...], hn[...]
    spec_re = jnp.concatenate([ur * hr - ui * hi, gr * hr + gi * hi, gr * ur + gi * ui], axis=0)
    spec_im = jnp.concatenate([ur * hi + ui * hr, gi * hr - gr * hi, gi * ur - gr * ui], axis=0)
    out = inverse(spec_re, spec_im, jnp.concatenate([un * hn, gn * hn, gn * un], axis=0), table, n)
    out, grad_taps[...] = out[: 2 * chans], out[2 * chans :].astype(BF16)
    grads[0] = (whole[2].astype(F32) * out[:chans]).astype(BF16)
    grads[1] = (out[chans:] * whole[1].astype(F32)).astype(BF16)
    grads[2] = (out[chans:] * whole[0].astype(F32)).astype(BF16)


def convolutions(me, pieces, table, taps_spec):
    chans, span = pieces[0].shape[-2:]
    n = N_CTX * span
    return pl.pallas_call(
        conv_kernel,
        out_shape=[like(3, chans, n), like(chans, n)],
        in_specs=[SCALAR] + [ON_CHIP] * (N_CTX + 7),
        out_specs=[ON_CHIP] * 2,
        scratch_shapes=[pltpu.VMEM((4, chans, n), BF16)],
        compiler_params=vmem(20),
        cost_estimate=pl.CostEstimate(flops=32 * chans * n * n, bytes_accessed=8 * MIB, transcendentals=0),
        name="convolutions",
    )(me, *pieces, *table, *taps_spec)


def gather_pieces(mine):
    along = [mine] + [shift_x(mine, s) for s in (1, 2, 3)]
    return along + [swap_core(a) for a in along]


def assemble_kernel(which, me, *refs):
    pieces, whole = refs[: len(which)], refs[-1]
    sub = pieces[0].shape[1]
    for p, piece in zip(which, pieces, strict=True):
        for b in range(3):
            whole[part_of(b * N_CTX + gathered_source(me[0], p), sub), :] = piece[b]


def assemble(me, pieces, which):
    _, sub, n = pieces[0].shape
    return pl.pallas_call(
        functools.partial(assemble_kernel, which),
        out_shape=like(3 * N_CTX * sub, n),
        in_specs=[SCALAR] + [ON_CHIP] * len(which),
        out_specs=ON_CHIP,
        compiler_params=vmem(8),
        name="assemble",
    )(me, *pieces)


def value_kernel(steps, which, me, *refs):
    weights, held, refs = refs[0], refs[1], refs[2:]
    pieces, refs = refs[: len(which)], refs[len(which) :]
    parts = refs[: len(steps)]
    whole = held
    if which:
        whole, far_whole, sem = refs[len(steps) :]
        assemble_kernel(which, me, *pieces, whole)
        copy = pltpu.make_async_copy(whole, far_whole, sem)
        copy.start()
    lhs = []
    for s in steps:
        at = (place(me, first=True) + s) % N_RING
        for k in range(N_RING):
            w = weights[group(me, at, k)]
            lhs.append(jnp.concatenate([w[b] for b in range(3)], axis=1))
    res = dot(jnp.concatenate(lhs, axis=0), whole[...]).astype(BF16)
    res = res.reshape(len(steps), *parts[0].shape)
    for i, part in enumerate(parts):
        part[...] = res[i]
    if which:
        copy.wait()


def value_part(me, weights, whole, steps, pieces=(), which=()):
    _, _, rows, width = weights.shape
    n = whole.shape[1]
    shapes = [like(N_RING, rows, n)] * len(steps)
    specs = [ON_CHIP] * len(steps)
    if which:
        shapes += [like(*whole.shape), pltpu.HBM(whole.shape, BF16)]
        specs += [ON_CHIP, FAR]
    return pl.pallas_call(
        functools.partial(value_kernel, steps, which),
        out_shape=shapes,
        in_specs=[SCALAR] + [ON_CHIP] * (len(which) + 2),
        out_specs=specs,
        scratch_shapes=[pltpu.SemaphoreType.DMA] if which else [],
        input_output_aliases={2: len(steps)} if which else {},
        compiler_params=vmem(16),
        cost_estimate=pl.CostEstimate(
            flops=24 * len(steps) * rows * width * n, bytes_accessed=2 * MIB, transcendentals=0
        ),
        name="value_part",
    )(me, weights, whole, *pieces)


def weight_kernel(steps, me, whole, *refs):
    feats, (out, res, sems) = refs[: len(steps)], refs[-3:]
    _, rows, n = feats[0].shape
    width = out.shape[-1]
    copies = []
    for i, s in enumerate(steps):
        at = (place(me, first=True) + N_RING - s) % N_RING
        tall = dot_t(feats[i][...].reshape(N_RING * rows, n), whole[...]).astype(BF16)
        for k in range(N_RING):
            for b in range(3):
                res[i, k, b] = tall[k * rows : (k + 1) * rows, b * width : (b + 1) * width]
            copies.append(pltpu.make_async_copy(res.at[i, k], out.at[group(me, at, k)], sems.at[i, k]))
            copies[-1].start()
    for copy in copies:
        copy.wait()


def weight_grad(me, whole, feats, steps, begun=None):
    _, rows, n = feats[0].shape
    width = whole.shape[0] // 3
    n_steps = len(steps)
    more = [] if begun is None else [begun]
    return pl.pallas_call(
        functools.partial(weight_kernel, steps),
        out_shape=pltpu.HBM((N_RING * N_RING, 3, rows, width), BF16),
        in_specs=[SCALAR] + [ON_CHIP] * (n_steps + 1) + [FAR] * len(more),
        out_specs=FAR,
        scratch_shapes=[
            pltpu.VMEM((n_steps, N_RING, 3, rows, width), BF16),
            pltpu.SemaphoreType.DMA((n_steps, N_RING)),
        ],
        input_output_aliases={n_steps + 2: 0} if more else {},
        compiler_params=vmem(18),
        cost_estimate=pl.CostEstimate(
            flops=24 * n_steps * rows * width * n, bytes_accessed=2 * MIB, transcendentals=0
        ),
        name="weight_grad",
    )(me, whole, *feats, *more)


def first_sum_kernel(me, *refs):
    parts, outs = refs[:N_RING], refs[N_RING:]
    for s in range(N_RING):
        k = pl.ds((place(me, first=False) + s) % N_RING, 1)
        total = parts[0][k].astype(F32)
        for i in range(1, N_RING):
            total = total + parts[i][k].astype(F32)
        outs[s][...] = total[0].astype(BF16)


def first_sum(me, parts):
    _, rows, n = parts[0].shape
    return pl.pallas_call(
        first_sum_kernel,
        out_shape=[like(rows, n)] * N_RING,
        in_specs=[SCALAR] + [ON_CHIP] * N_RING,
        out_specs=[ON_CHIP] * N_RING,
        compiler_params=vmem(6),
        name="first_sum",
    )(me, *parts)


def sum_kernel(me, *refs):
    parts, outs, whole = refs[:N_RING], refs[N_RING:-1], refs[-1]
    total = parts[0][...].astype(F32)
    for i in range(1, N_RING):
        total = total + parts[i][...].astype(F32)
    whole[...] = total.astype(BF16)
    tokens = outs[0].shape[-1]
    for ahead in range(N_X):
        for other in range(2):
            outs[ahead][other] = whole[:, part_of(target(me[0], ahead, other), tokens)]


def sum_parts(me, parts):
    rows, n = parts[0].shape
    return pl.pallas_call(
        sum_kernel,
        out_shape=[like(2, rows, n // N_CTX)] * N_X,
        in_specs=[SCALAR] + [ON_CHIP] * N_RING,
        out_specs=[ON_CHIP] * N_X,
        scratch_shapes=[pltpu.VMEM((rows, n), BF16)],
        compiler_params=vmem(6),
        name="sum_parts",
    )(me, *parts)


def finish_kernel(me, *refs):
    pieces, out, whole = refs[:N_CTX], refs[N_CTX], refs[N_CTX + 1]
    sub = pieces[0].shape[0]
    for p in range(N_CTX):
        whole[part_of(source(me[0], p), sub), :] = pieces[p][...]
    out[...] = whole[...].T


def finish(me, pieces):
    rows, tokens = pieces[0].shape
    return pl.pallas_call(
        finish_kernel,
        out_shape=like(tokens, rows * N_CTX),
        in_specs=[SCALAR] + [ON_CHIP] * N_CTX,
        scratch_shapes=[pltpu.VMEM((rows * N_CTX, tokens), BF16)],
        compiler_params=vmem(6),
        name="finish",
    )(me, *pieces)


def tie(a, b):
    return lax.optimization_barrier((a, b))


def per_device(features_in, w_featurizer, filter_taps, query_proj, key_proj, value_proj, grad_mixed):
    width_dev = features_in.shape[1]
    me = jnp.stack([lax.axis_index("ctx"), lax.axis_index("tp")]).astype(jnp.int32)
    weights = w_featurizer.transpose(0, 2, 1, 3)
    ready = prepare(me, (key_proj, value_proj, grad_mixed, query_proj, features_in))
    along = [ready[0]] + [shift_x(ready[s], s) for s in (1, 2, 3)]
    spec_taps = taps_spectrum(filter_taps.reshape(width_dev // N_CTX, -1))
    along, spec_taps = tie(along, spec_taps)
    *table, hr, hi, hn = spec_taps
    pieces = [a[0] for a in along] + [swap_core(a[1]) for a in along]
    grads, grad_taps = convolutions(me, pieces, table, (hr, hi, hn))
    own, sibling, next1, next2 = gather_start(grads)
    sibling, pieces = tie(sibling, pieces)
    last = spin(next1)
    feats = join_features(me, pieces)
    feats = [feats] + [shift_ring(feats, s, first=False) for s in (1, 2, 3)]
    last, feats = tie(last, feats)
    pieces = (own, sibling, next1, next2, swap_core(next1), swap_core(next2))
    whole = assemble(me, pieces, (0, 1, 2, 3, 5, 6))
    *sent, whole, far_whole = value_part(me, weights, whole, (1, 2, 3), (last, swap_core(last)), (4, 7))
    parts = [shift_ring(p, s, first=True) for p, s in zip(sent, (1, 2, 3), strict=True)]
    feats = stack(me, feats)
    feats1, feats3 = shift_ring(feats, 1, first=True), shift_ring(feats, 3, first=True)
    parts = [*value_part(me, weights, whole, (0,)), *parts]
    parts = first_sum(me, parts)
    parts, (feats1, feats3) = tie(parts, (feats1, feats3))
    parts = [parts[0]] + [shift_ring(parts[s], s, first=False) for s in (1, 2, 3)]
    feats = [feats, feats1, shift_ring(feats, 2, first=True), feats3]
    grad_w = weight_grad(me, far_whole, [feats[s] for s in (0, 1, 3)], (0, 1, 3))
    parts, grad_w = tie(parts, grad_w)
    ready = sum_parts(me, parts)
    along = [ready[0]] + [shift_x(ready[s], s) for s in (1, 2, 3)]
    grad_w = weight_grad(me, far_whole, [feats[2]], (2,), grad_w)
    along, grad_w = tie(along, grad_w)
    grad_features = finish(me, [a[0] for a in along] + [swap_core(a[1]) for a in along])
    return grad_features, grad_w.transpose(0, 2, 1, 3), grad_taps.reshape(filter_taps.shape)


def solution(mesh):
    return jax.shard_map(
        per_device,
        mesh=mesh,
        in_specs=(
            P("ctx", "tp"),
            P(None, "ctx", None, "tp"),
            P("tp", "ctx", None),
            P("ctx", "tp"),
            P("ctx", "tp"),
            P("ctx", "tp"),
            P("ctx", "tp"),
        ),
        out_specs=(P("ctx", "tp"), P(None, "ctx", None, "tp"), P("tp", "ctx", None)),
        check_vma=False,
    )
```

```python
import functools
import math

import jax
import jax.numpy as jnp
import numpy as np
from jax import lax
from jax.experimental import pallas as pl
from jax.experimental.pallas import tpu as pltpu
from jax.sharding import PartitionSpec as P

BF16 = jnp.bfloat16
F32 = jnp.float32
N_X = 4
N_CTX = 8
N_RING = 4
MIB = 1024 * 1024
ON_CHIP = pl.BlockSpec(memory_space=pltpu.VMEM)
FAR = pl.BlockSpec(memory_space=pltpu.HBM)
SCALAR = pl.BlockSpec(memory_space=pltpu.SMEM)


def vmem(mib):
    return pltpu.CompilerParams(vmem_limit_bytes=mib * MIB)


def like(*shape, dtype=BF16):
    return jax.ShapeDtypeStruct(shape, dtype)


def tables(n):
    idx = np.arange(n, dtype=np.int64)
    angle = (np.outer(idx, idx) % (2 * n)).astype(np.float64) * (math.pi / n)
    return [jnp.asarray(whole.astype(BF16)) for whole in (np.cos(angle), np.sin(angle))]


def dot(a, b):
    return lax.dot_general(a, b, (((1,), (0,)), ((), ())), preferred_element_type=F32)


def dot_t(a, b):
    return lax.dot_general(a, b, (((1,), (1,)), ((), ())), preferred_element_type=F32)


def shift_x(a, steps):
    return lax.ppermute(a, "ctx", [(i, (i + 2 * steps) % N_CTX) for i in range(N_CTX)])


def swap_core(a):
    return lax.ppermute(a, "ctx", [(i, i ^ 1) for i in range(N_CTX)])


def source(me, piece):
    back, other = piece % N_X, piece // N_X
    chip = (me // 2 + N_X - back) % N_X
    core = me % 2
    return 2 * chip + (1 - core if other else core)


def spin(a):
    pairs = [(2 * x + core, 2 * ((x + 1 - 2 * core) % N_X) + core) for x in range(N_X) for core in range(2)]
    return lax.ppermute(a, "ctx", pairs)


def gather_start(mine):
    sibling = swap_core(mine)
    return [mine, sibling, spin(mine), spin(sibling)]


def gathered_source(me, piece):
    chip, core = me // 2, me % 2
    if piece < 2:
        return 2 * chip + (core if piece == 0 else 1 - core)
    kind, theirs = (piece - 2) % 3, piece >= 5
    back = 1 - 2 * core
    if theirs:
        back, core = -back, 1 - core
    chip = (chip + N_X - (2 if kind == 2 else back)) % N_X
    return 2 * chip + (1 - core if kind == 1 else core)


def target(me, ahead, other):
    chip = (me // 2 + ahead) % N_X
    core = me % 2
    return 2 * chip + (1 - core if other else core)


def place(me, first):
    on_y, on_z = me[1] // N_RING, me[1] % N_RING
    return jnp.where((me[0] % 2 == 0) == first, on_y, on_z)


def group(me, at, k):
    return jnp.where(me[0] % 2 == 0, at * N_RING + k, k * N_RING + at)


def shift_ring(a, steps, first):
    pairs = []
    for ctx in range(N_CTX):
        for y in range(N_RING):
            for z in range(N_RING):
                along_y = (ctx % 2 == 0) == first
                to = ((y + steps) % N_RING, z) if along_y else (y, (z + steps) % N_RING)
                base = ctx * N_RING * N_RING
                pairs.append((base + y * N_RING + z, base + to[0] * N_RING + to[1]))
    return lax.ppermute(a, ("ctx", "tp"), pairs)


def part_of(index, size):
    return pl.ds(pl.multiple_of(index * size, size), size)


def prep_kernel(me, *refs):
    n_arr = len(refs) - 3 - N_X
    arrays, outs = refs[:n_arr], refs[n_arr : n_arr + N_X]
    local, turned, sems = refs[n_arr + N_X :]
    copies = [pltpu.make_async_copy(arrays[a], local.at[a], sems.at[a]) for a in range(n_arr)]
    for copy in copies:
        copy.start()
    sub = outs[0].shape[2]
    for a in range(n_arr):
        copies[a].wait()
        turned[a] = local[a].T
    for ahead in range(N_X):
        for other in range(2):
            rows = part_of(target(me[0], ahead, other), sub)
            for a in range(n_arr):
                outs[ahead][other, a] = turned[a, rows, :]


def prepare(me, arrays):
    tokens, width = arrays[0].shape
    n_arr = len(arrays)
    return pl.pallas_call(
        prep_kernel,
        out_shape=[like(2, n_arr, width // N_CTX, tokens)] * N_X,
        in_specs=[SCALAR] + [FAR] * n_arr,
        out_specs=[ON_CHIP] * N_X,
        scratch_shapes=[
            pltpu.VMEM((n_arr, tokens, width), BF16),
            pltpu.VMEM((n_arr, width, tokens), BF16),
            pltpu.SemaphoreType.DMA((n_arr,)),
        ],
        compiler_params=vmem(6),
        name="prepare",
    )(me, *[pltpu.with_memory_space_constraint(a, pltpu.HBM) for a in arrays])


def join_kernel(me, *refs):
    pieces, out = refs[:N_CTX], refs[N_CTX]
    span = pieces[0].shape[-1]
    for p in range(N_CTX):
        out[:, part_of(source(me[0], p), span)] = pieces[p][pieces[p].shape[0] - 1]


def join_features(me, pieces):
    _, sub, span = pieces[0].shape
    return pl.pallas_call(
        join_kernel,
        out_shape=like(sub, span * N_CTX),
        in_specs=[SCALAR] + [ON_CHIP] * N_CTX,
        out_specs=ON_CHIP,
        compiler_params=vmem(6),
        name="join_features",
    )(me, *pieces)


def stack_kernel(me, *refs):
    pieces, out = refs[:N_RING], refs[N_RING]
    for s in range(N_RING):
        out[pl.ds((place(me, first=False) + N_RING - s) % N_RING, 1)] = pieces[s][...][None]


def stack(me, pieces):
    return pl.pallas_call(
        stack_kernel,
        out_shape=like(N_RING, *pieces[0].shape),
        in_specs=[SCALAR] + [ON_CHIP] * N_RING,
        out_specs=ON_CHIP,
        compiler_params=vmem(6),
        name="stack_features",
    )(me, *pieces)


def signs(n):
    lane = lax.broadcasted_iota(jnp.int32, (1, n), 1)
    return jnp.where(lane % 2 == 0, 1.0, -1.0).astype(F32)


def spectrum(signals, table, n):
    nyq = jnp.sum(signals.astype(F32) * signs(n), axis=1, keepdims=True)
    return dot(signals, table[0][...]), dot(signals, table[1][...]), nyq


def split(a):
    high = a.astype(BF16)
    return high, (a - high.astype(F32)).astype(BF16)


def inverse(re, im, nyq, table, n):
    rows = re.shape[0]
    lane = lax.broadcasted_iota(jnp.int32, (1, n), 1)
    weight = jnp.where(lane == 0, 0.5 / n, 1.0 / n).astype(F32)
    re_hi, re_lo = split(re * weight)
    im_hi, im_lo = split(im * weight)
    both = dot(jnp.concatenate([re_hi, re_lo], axis=0), table[0][...])
    both = both + dot(jnp.concatenate([im_hi, im_lo], axis=0), table[1][...])
    return both[:rows] + both[rows:] + (nyq * (0.5 / n)) * signs(n)


def taps_kernel(*refs):
    far, taps = refs[:2], refs[2]
    table, (re, im, nyq, sems) = refs[3:5], refs[5:]
    copies = [pltpu.make_async_copy(far[i], table[i], sems.at[i]) for i in range(2)]
    for copy in copies:
        copy.start()
    for copy in copies:
        copy.wait()
    re[...], im[...], nyq[...] = spectrum(taps[...], table, taps.shape[1])


def taps_spectrum(taps):
    chans, n = taps.shape
    return pl.pallas_call(
        taps_kernel,
        out_shape=[like(n, n)] * 2 + [like(chans, n, dtype=F32)] * 2 + [like(chans, 1, dtype=F32)],
        in_specs=[FAR] * 2 + [ON_CHIP],
        out_specs=[ON_CHIP] * 5,
        scratch_shapes=[pltpu.SemaphoreType.DMA((2,))],
        compiler_params=vmem(12),
        cost_estimate=pl.CostEstimate(flops=8 * chans * n * n, bytes_accessed=8 * MIB, transcendentals=0),
        name="taps_spectrum",
    )(*[pltpu.with_memory_space_constraint(t, pltpu.HBM) for t in tables(n)], taps)


def conv_kernel(me, *refs):
    pieces = refs[:N_CTX]
    table = refs[N_CTX : N_CTX + 2]
    hr, hi, hn = refs[N_CTX + 2 : N_CTX + 5]
    grads, grad_taps, whole = refs[N_CTX + 5 :]
    chans, span = pieces[0].shape[-2:]
    n = N_CTX * span
    for p in range(N_CTX):
        for a in range(4):
            whole[a, :, part_of(source(me[0], p), span)] = pieces[p][a]
    product = (whole[0].astype(F32) * whole[1].astype(F32)).astype(BF16)
    grad_conv = (whole[2].astype(F32) * whole[3].astype(F32)).astype(BF16)
    re, im, nyq = spectrum(jnp.concatenate([product, grad_conv], axis=0), table, n)
    ur, gr, ui, gi, un, gn = re[:chans], re[chans:], im[:chans], im[chans:], nyq[:chans], nyq[chans:]
    hr, hi, hn = hr[...], hi[...], hn[...]
    spec_re = jnp.concatenate([ur * hr - ui * hi, gr * hr + gi * hi, gr * ur + gi * ui], axis=0)
    spec_im = jnp.concatenate([ur * hi + ui * hr, gi * hr - gr * hi, gi * ur - gr * ui], axis=0)
    out = inverse(spec_re, spec_im, jnp.concatenate([un * hn, gn * hn, gn * un], axis=0), table, n)
    out, grad_taps[...] = out[: 2 * chans], out[2 * chans :].astype(BF16)
    grads[0] = (whole[2].astype(F32) * out[:chans]).astype(BF16)
    grads[1] = (out[chans:] * whole[1].astype(F32)).astype(BF16)
    grads[2] = (out[chans:] * whole[0].astype(F32)).astype(BF16)


def convolutions(me, pieces, table, taps_spec):
    chans, span = pieces[0].shape[-2:]
    n = N_CTX * span
    return pl.pallas_call(
        conv_kernel,
        out_shape=[like(3, chans, n), like(chans, n)],
        in_specs=[SCALAR] + [ON_CHIP] * (N_CTX + 5),
        out_specs=[ON_CHIP] * 2,
        scratch_shapes=[pltpu.VMEM((4, chans, n), BF16)],
        compiler_params=vmem(20),
        cost_estimate=pl.CostEstimate(flops=32 * chans * n * n, bytes_accessed=8 * MIB, transcendentals=0),
        name="convolutions",
    )(me, *pieces, *table, *taps_spec)


def gather_pieces(mine):
    along = [mine] + [shift_x(mine, s) for s in (1, 2, 3)]
    return along + [swap_core(a) for a in along]


def assemble_kernel(which, me, *refs):
    pieces, whole = refs[: len(which)], refs[-1]
    sub = pieces[0].shape[1]
    for p, piece in zip(which, pieces, strict=True):
        for b in range(3):
            whole[part_of(b * N_CTX + gathered_source(me[0], p), sub), :] = piece[b]


def assemble(me, pieces, which):
    _, sub, n = pieces[0].shape
    return pl.pallas_call(
        functools.partial(assemble_kernel, which),
        out_shape=like(3 * N_CTX * sub, n),
        in_specs=[SCALAR] + [ON_CHIP] * len(which),
        out_specs=ON_CHIP,
        compiler_params=vmem(8),
        name="assemble",
    )(me, *pieces)


def value_kernel(steps, which, me, *refs):
    weights, held, refs = refs[0], refs[1], refs[2:]
    pieces, refs = refs[: len(which)], refs[len(which) :]
    parts = refs[: len(steps)]
    whole = held
    if which:
        whole, far_whole, sem = refs[len(steps) :]
        assemble_kernel(which, me, *pieces, whole)
        copy = pltpu.make_async_copy(whole, far_whole, sem)
        copy.start()
    lhs = []
    for s in steps:
        at = (place(me, first=True) + s) % N_RING
        for k in range(N_RING):
            w = weights[group(me, at, k)]
            lhs.append(jnp.concatenate([w[b] for b in range(3)], axis=1))
    res = dot(jnp.concatenate(lhs, axis=0), whole[...]).astype(BF16)
    res = res.reshape(len(steps), *parts[0].shape)
    for i, part in enumerate(parts):
        part[...] = res[i]
    if which:
        copy.wait()


def value_part(me, weights, whole, steps, pieces=(), which=()):
    _, _, rows, width = weights.shape
    n = whole.shape[1]
    shapes = [like(N_RING, rows, n)] * len(steps)
    specs = [ON_CHIP] * len(steps)
    if which:
        shapes += [like(*whole.shape), pltpu.HBM(whole.shape, BF16)]
        specs += [ON_CHIP, FAR]
    return pl.pallas_call(
        functools.partial(value_kernel, steps, which),
        out_shape=shapes,
        in_specs=[SCALAR] + [ON_CHIP] * (len(which) + 2),
        out_specs=specs,
        scratch_shapes=[pltpu.SemaphoreType.DMA] if which else [],
        input_output_aliases={2: len(steps)} if which else {},
        compiler_params=vmem(16),
        cost_estimate=pl.CostEstimate(
            flops=24 * len(steps) * rows * width * n, bytes_accessed=2 * MIB, transcendentals=0
        ),
        name="value_part",
    )(me, weights, whole, *pieces)


def weight_kernel(steps, me, whole, *refs):
    feats, (out, res, sems) = refs[: len(steps)], refs[-3:]
    _, rows, n = feats[0].shape
    width = out.shape[-1]
    copies = []
    for i, s in enumerate(steps):
        at = (place(me, first=True) + N_RING - s) % N_RING
        tall = dot_t(feats[i][...].reshape(N_RING * rows, n), whole[...]).astype(BF16)
        for k in range(N_RING):
            for b in range(3):
                res[i, k, b] = tall[k * rows : (k + 1) * rows, b * width : (b + 1) * width]
            copies.append(pltpu.make_async_copy(res.at[i, k], out.at[group(me, at, k)], sems.at[i, k]))
            copies[-1].start()
    for copy in copies:
        copy.wait()


def weight_grad(me, whole, feats, steps, begun=None):
    _, rows, n = feats[0].shape
    width = whole.shape[0] // 3
    n_steps = len(steps)
    more = [] if begun is None else [begun]
    return pl.pallas_call(
        functools.partial(weight_kernel, steps),
        out_shape=pltpu.HBM((N_RING * N_RING, 3, rows, width), BF16),
        in_specs=[SCALAR] + [ON_CHIP] * (n_steps + 1) + [FAR] * len(more),
        out_specs=FAR,
        scratch_shapes=[
            pltpu.VMEM((n_steps, N_RING, 3, rows, width), BF16),
            pltpu.SemaphoreType.DMA((n_steps, N_RING)),
        ],
        input_output_aliases={n_steps + 2: 0} if more else {},
        compiler_params=vmem(18),
        cost_estimate=pl.CostEstimate(
            flops=24 * n_steps * rows * width * n, bytes_accessed=2 * MIB, transcendentals=0
        ),
        name="weight_grad",
    )(me, whole, *feats, *more)


def first_sum_kernel(me, *refs):
    parts, outs = refs[:N_RING], refs[N_RING:]
    for s in range(N_RING):
        k = pl.ds((place(me, first=False) + s) % N_RING, 1)
        total = parts[0][k].astype(F32)
        for i in range(1, N_RING):
            total = total + parts[i][k].astype(F32)
        outs[s][...] = total[0].astype(BF16)


def first_sum(me, parts):
    _, rows, n = parts[0].shape
    return pl.pallas_call(
        first_sum_kernel,
        out_shape=[like(rows, n)] * N_RING,
        in_specs=[SCALAR] + [ON_CHIP] * N_RING,
        out_specs=[ON_CHIP] * N_RING,
        compiler_params=vmem(6),
        name="first_sum",
    )(me, *parts)


def sum_kernel(me, *refs):
    parts, outs, whole = refs[:N_RING], refs[N_RING:-1], refs[-1]
    total = parts[0][...].astype(F32)
    for i in range(1, N_RING):
        total = total + parts[i][...].astype(F32)
    whole[...] = total.astype(BF16)
    tokens = outs[0].shape[-1]
    for ahead in range(N_X):
        for other in range(2):
            outs[ahead][other] = whole[:, part_of(target(me[0], ahead, other), tokens)]


def sum_parts(me, parts):
    rows, n = parts[0].shape
    return pl.pallas_call(
        sum_kernel,
        out_shape=[like(2, rows, n // N_CTX)] * N_X,
        in_specs=[SCALAR] + [ON_CHIP] * N_RING,
        out_specs=[ON_CHIP] * N_X,
        scratch_shapes=[pltpu.VMEM((rows, n), BF16)],
        compiler_params=vmem(6),
        name="sum_parts",
    )(me, *parts)


def finish_kernel(me, *refs):
    pieces, out, whole = refs[:N_CTX], refs[N_CTX], refs[N_CTX + 1]
    sub = pieces[0].shape[0]
    for p in range(N_CTX):
        whole[part_of(source(me[0], p), sub), :] = pieces[p][...]
    out[...] = whole[...].T


def finish(me, pieces):
    rows, tokens = pieces[0].shape
    return pl.pallas_call(
        finish_kernel,
        out_shape=like(tokens, rows * N_CTX),
        in_specs=[SCALAR] + [ON_CHIP] * N_CTX,
        scratch_shapes=[pltpu.VMEM((rows * N_CTX, tokens), BF16)],
        compiler_params=vmem(6),
        name="finish",
    )(me, *pieces)


def tie(a, b):
    return lax.optimization_barrier((a, b))


def per_device(features_in, w_featurizer, filter_taps, query_proj, key_proj, value_proj, grad_mixed):
    width_dev = features_in.shape[1]
    me = jnp.stack([lax.axis_index("ctx"), lax.axis_index("tp")]).astype(jnp.int32)
    weights = w_featurizer.transpose(0, 2, 1, 3)
    ready = prepare(me, (key_proj, value_proj, grad_mixed, query_proj, features_in))
    along = [ready[0]] + [shift_x(ready[s], s) for s in (1, 2, 3)]
    spec_taps = taps_spectrum(filter_taps.reshape(width_dev // N_CTX, -1))
    along, spec_taps = tie(along, spec_taps)
    *table, hr, hi, hn = spec_taps
    pieces = [a[0] for a in along] + [swap_core(a[1]) for a in along]
    grads, grad_taps = convolutions(me, pieces, table, (hr, hi, hn))
    own, sibling, next1, next2 = gather_start(grads)
    sibling, pieces = tie(sibling, pieces)
    last = spin(next1)
    feats = join_features(me, pieces)
    feats = [feats] + [shift_ring(feats, s, first=False) for s in (1, 2, 3)]
    last, feats = tie(last, feats)
    pieces = (own, sibling, next1, next2, swap_core(next1), swap_core(next2))
    whole = assemble(me, pieces, (0, 1, 2, 3, 5, 6))
    *sent, whole, far_whole = value_part(me, weights, whole, (1, 2, 3), (last, swap_core(last)), (4, 7))
    parts = [shift_ring(p, s, first=True) for p, s in zip(sent, (1, 2, 3), strict=True)]
    feats = stack(me, feats)
    feats1, feats3 = shift_ring(feats, 1, first=True), shift_ring(feats, 3, first=True)
    (part,) = value_part(me, weights, whole, (0,))
    part, feats = tie(part, feats)
    parts = [part, *parts]
    parts = first_sum(me, parts)
    parts, (feats1, feats3) = tie(parts, (feats1, feats3))
    parts = [parts[0]] + [shift_ring(parts[s], s, first=False) for s in (1, 2, 3)]
    feats = [feats, feats1, shift_ring(feats, 2, first=True), feats3]
    grad_w = weight_grad(me, far_whole, [feats[s] for s in (0, 1, 3)], (0, 1, 3))
    parts, grad_w = tie(parts, grad_w)
    ready = sum_parts(me, parts)
    along = [ready[0]] + [shift_x(ready[s], s) for s in (1, 2, 3)]
    grad_w = weight_grad(me, far_whole, [feats[2]], (2,), grad_w)
    along, grad_w = tie(along, grad_w)
    grad_features = finish(me, [a[0] for a in along] + [swap_core(a[1]) for a in along])
    return grad_features, grad_w.transpose(0, 2, 1, 3), grad_taps.reshape(filter_taps.shape)


def solution(mesh):
    return jax.shard_map(
        per_device,
        mesh=mesh,
        in_specs=(
            P("ctx", "tp"),
            P(None, "ctx", None, "tp"),
            P("tp", "ctx", None),
            P("ctx", "tp"),
            P("ctx", "tp"),
            P("ctx", "tp"),
            P("ctx", "tp"),
        ),
        out_specs=(P("ctx", "tp"), P(None, "ctx", None, "tp"), P("tp", "ctx", None)),
        check_vma=False,
    )
```

```python
import functools
import math

import jax
import jax.numpy as jnp
import numpy as np
from jax import lax
from jax.experimental import pallas as pl
from jax.experimental.pallas import tpu as pltpu
from jax.sharding import PartitionSpec as P

BF16 = jnp.bfloat16
F32 = jnp.float32
N_X = 4
N_CTX = 8
N_RING = 4
MIB = 1024 * 1024
ON_CHIP = pl.BlockSpec(memory_space=pltpu.VMEM)
FAR = pl.BlockSpec(memory_space=pltpu.HBM)
SCALAR = pl.BlockSpec(memory_space=pltpu.SMEM)


def vmem(mib):
    return pltpu.CompilerParams(vmem_limit_bytes=mib * MIB)


def like(*shape, dtype=BF16):
    return jax.ShapeDtypeStruct(shape, dtype)


def tables(n):
    idx = np.arange(n, dtype=np.int64)
    angle = (np.outer(idx, idx) % (2 * n)).astype(np.float64) * (math.pi / n)
    return [jnp.asarray(whole.astype(BF16)) for whole in (np.cos(angle), np.sin(angle))]


def dot(a, b):
    return lax.dot_general(a, b, (((1,), (0,)), ((), ())), preferred_element_type=F32)


def dot_t(a, b):
    return lax.dot_general(a, b, (((1,), (1,)), ((), ())), preferred_element_type=F32)


def shift_x(a, steps):
    return lax.ppermute(a, "ctx", [(i, (i + 2 * steps) % N_CTX) for i in range(N_CTX)])


def swap_core(a):
    return lax.ppermute(a, "ctx", [(i, i ^ 1) for i in range(N_CTX)])


def source(me, piece):
    back, other = piece % N_X, piece // N_X
    chip = (me // 2 + N_X - back) % N_X
    core = me % 2
    return 2 * chip + (1 - core if other else core)


def spin(a):
    pairs = [(2 * x + core, 2 * ((x + 1 - 2 * core) % N_X) + core) for x in range(N_X) for core in range(2)]
    return lax.ppermute(a, "ctx", pairs)


def gather_start(mine):
    sibling = swap_core(mine)
    return [mine, sibling, spin(mine), spin(sibling)]


def gathered_source(me, piece):
    chip, core = me // 2, me % 2
    if piece < 2:
        return 2 * chip + (core if piece == 0 else 1 - core)
    kind, theirs = (piece - 2) % 3, piece >= 5
    back = 1 - 2 * core
    if theirs:
        back, core = -back, 1 - core
    chip = (chip + N_X - (2 if kind == 2 else back)) % N_X
    return 2 * chip + (1 - core if kind == 1 else core)


def target(me, ahead, other):
    chip = (me // 2 + ahead) % N_X
    core = me % 2
    return 2 * chip + (1 - core if other else core)


def place(me, first):
    on_y, on_z = me[1] // N_RING, me[1] % N_RING
    return jnp.where((me[0] % 2 == 0) == first, on_y, on_z)


def group(me, at, k):
    return jnp.where(me[0] % 2 == 0, at * N_RING + k, k * N_RING + at)


def shift_ring(a, steps, first):
    pairs = []
    for ctx in range(N_CTX):
        for y in range(N_RING):
            for z in range(N_RING):
                along_y = (ctx % 2 == 0) == first
                to = ((y + steps) % N_RING, z) if along_y else (y, (z + steps) % N_RING)
                base = ctx * N_RING * N_RING
                pairs.append((base + y * N_RING + z, base + to[0] * N_RING + to[1]))
    return lax.ppermute(a, ("ctx", "tp"), pairs)


def part_of(index, size):
    return pl.ds(pl.multiple_of(index * size, size), size)


def prep_kernel(me, *refs):
    n_arr = len(refs) - 3 - N_X
    arrays, outs = refs[:n_arr], refs[n_arr : n_arr + N_X]
    local, turned, sems = refs[n_arr + N_X :]
    copies = [pltpu.make_async_copy(arrays[a], local.at[a], sems.at[a]) for a in range(n_arr)]
    for copy in copies:
        copy.start()
    sub = outs[0].shape[2]
    for a in range(n_arr):
        copies[a].wait()
        turned[a] = local[a].T
    for ahead in range(N_X):
        for other in range(2):
            rows = part_of(target(me[0], ahead, other), sub)
            for a in range(n_arr):
                outs[ahead][other, a] = turned[a, rows, :]


def prepare(me, arrays):
    tokens, width = arrays[0].shape
    n_arr = len(arrays)
    return pl.pallas_call(
        prep_kernel,
        out_shape=[like(2, n_arr, width // N_CTX, tokens)] * N_X,
        in_specs=[SCALAR] + [FAR] * n_arr,
        out_specs=[ON_CHIP] * N_X,
        scratch_shapes=[
            pltpu.VMEM((n_arr, tokens, width), BF16),
            pltpu.VMEM((n_arr, width, tokens), BF16),
            pltpu.SemaphoreType.DMA((n_arr,)),
        ],
        compiler_params=vmem(6),
        name="prepare",
    )(me, *[pltpu.with_memory_space_constraint(a, pltpu.HBM) for a in arrays])


def join_kernel(me, *refs):
    pieces, out = refs[:N_CTX], refs[N_CTX]
    span = pieces[0].shape[-1]
    for p in range(N_CTX):
        out[:, part_of(source(me[0], p), span)] = pieces[p][pieces[p].shape[0] - 1]


def join_features(me, pieces):
    _, sub, span = pieces[0].shape
    return pl.pallas_call(
        join_kernel,
        out_shape=like(sub, span * N_CTX),
        in_specs=[SCALAR] + [ON_CHIP] * N_CTX,
        out_specs=ON_CHIP,
        compiler_params=vmem(6),
        name="join_features",
    )(me, *pieces)


def stack_kernel(me, *refs):
    pieces, out = refs[:N_RING], refs[N_RING]
    for s in range(N_RING):
        out[pl.ds((place(me, first=False) + N_RING - s) % N_RING, 1)] = pieces[s][...][None]


def stack(me, pieces):
    return pl.pallas_call(
        stack_kernel,
        out_shape=like(N_RING, *pieces[0].shape),
        in_specs=[SCALAR] + [ON_CHIP] * N_RING,
        out_specs=ON_CHIP,
        compiler_params=vmem(6),
        name="stack_features",
    )(me, *pieces)


def signs(n):
    lane = lax.broadcasted_iota(jnp.int32, (1, n), 1)
    return jnp.where(lane % 2 == 0, 1.0, -1.0).astype(F32)


def spectrum(signals, table, n):
    nyq = jnp.sum(signals.astype(F32) * signs(n), axis=1, keepdims=True)
    return dot(signals, table[0][...]), dot(signals, table[1][...]), nyq


def split(a):
    high = a.astype(BF16)
    return high, (a - high.astype(F32)).astype(BF16)


def inverse(re, im, nyq, table, n):
    rows = re.shape[0]
    lane = lax.broadcasted_iota(jnp.int32, (1, n), 1)
    weight = jnp.where(lane == 0, 0.5 / n, 1.0 / n).astype(F32)
    re_hi, re_lo = split(re * weight)
    im_hi, im_lo = split(im * weight)
    both = dot(jnp.concatenate([re_hi, re_lo], axis=0), table[0][...])
    both = both + dot(jnp.concatenate([im_hi, im_lo], axis=0), table[1][...])
    return both[:rows] + both[rows:] + (nyq * (0.5 / n)) * signs(n)


def taps_kernel(*refs):
    far, taps = refs[:2], refs[2]
    table, (re, im, nyq, sems) = refs[3:5], refs[5:]
    copies = [pltpu.make_async_copy(far[i], table[i], sems.at[i]) for i in range(2)]
    for copy in copies:
        copy.start()
    for copy in copies:
        copy.wait()
    re[...], im[...], nyq[...] = spectrum(taps[...], table, taps.shape[1])


def taps_spectrum(taps):
    chans, n = taps.shape
    return pl.pallas_call(
        taps_kernel,
        out_shape=[like(n, n)] * 2 + [like(chans, n, dtype=F32)] * 2 + [like(chans, 1, dtype=F32)],
        in_specs=[FAR] * 2 + [ON_CHIP],
        out_specs=[ON_CHIP] * 5,
        scratch_shapes=[pltpu.SemaphoreType.DMA((2,))],
        compiler_params=vmem(12),
        cost_estimate=pl.CostEstimate(flops=8 * chans * n * n, bytes_accessed=8 * MIB, transcendentals=0),
        name="taps_spectrum",
    )(*[pltpu.with_memory_space_constraint(t, pltpu.HBM) for t in tables(n)], taps)


def conv_kernel(me, *refs):
    pieces = refs[:N_CTX]
    table = refs[N_CTX : N_CTX + 2]
    hr, hi, hn = refs[N_CTX + 2 : N_CTX + 5]
    grads, grad_taps, whole = refs[N_CTX + 5 :]
    chans, span = pieces[0].shape[-2:]
    n = N_CTX * span
    for p in range(N_CTX):
        for a in range(4):
            whole[a, :, part_of(source(me[0], p), span)] = pieces[p][a]
    product = (whole[0].astype(F32) * whole[1].astype(F32)).astype(BF16)
    grad_conv = (whole[2].astype(F32) * whole[3].astype(F32)).astype(BF16)
    re, im, nyq = spectrum(jnp.concatenate([product, grad_conv], axis=0), table, n)
    ur, gr, ui, gi, un, gn = re[:chans], re[chans:], im[:chans], im[chans:], nyq[:chans], nyq[chans:]
    hr, hi, hn = hr[...], hi[...], hn[...]
    spec_re = jnp.concatenate([ur * hr - ui * hi, gr * hr + gi * hi, gr * ur + gi * ui], axis=0)
    spec_im = jnp.concatenate([ur * hi + ui * hr, gi * hr - gr * hi, gi * ur - gr * ui], axis=0)
    out = inverse(spec_re, spec_im, jnp.concatenate([un * hn, gn * hn, gn * un], axis=0), table, n)
    out, grad_taps[...] = out[: 2 * chans], out[2 * chans :].astype(BF16)
    grads[0] = (whole[2].astype(F32) * out[:chans]).astype(BF16)
    grads[1] = (out[chans:] * whole[1].astype(F32)).astype(BF16)
    grads[2] = (out[chans:] * whole[0].astype(F32)).astype(BF16)


def convolutions(me, pieces, table, taps_spec):
    chans, span = pieces[0].shape[-2:]
    n = N_CTX * span
    return pl.pallas_call(
        conv_kernel,
        out_shape=[like(3, chans, n), like(chans, n)],
        in_specs=[SCALAR] + [ON_CHIP] * (N_CTX + 5),
        out_specs=[ON_CHIP] * 2,
        scratch_shapes=[pltpu.VMEM((4, chans, n), BF16)],
        compiler_params=vmem(20),
        cost_estimate=pl.CostEstimate(flops=32 * chans * n * n, bytes_accessed=8 * MIB, transcendentals=0),
        name="convolutions",
    )(me, *pieces, *table, *taps_spec)


def gather_pieces(mine):
    along = [mine] + [shift_x(mine, s) for s in (1, 2, 3)]
    return along + [swap_core(a) for a in along]


def assemble_kernel(which, me, *refs):
    pieces, whole = refs[: len(which)], refs[-1]
    sub = pieces[0].shape[1]
    for p, piece in zip(which, pieces, strict=True):
        for b in range(3):
            whole[part_of(b * N_CTX + gathered_source(me[0], p), sub), :] = piece[b]


def assemble(me, pieces, which):
    _, sub, n = pieces[0].shape
    return pl.pallas_call(
        functools.partial(assemble_kernel, which),
        out_shape=like(3 * N_CTX * sub, n),
        in_specs=[SCALAR] + [ON_CHIP] * len(which),
        out_specs=ON_CHIP,
        compiler_params=vmem(8),
        name="assemble",
    )(me, *pieces)


def value_kernel(steps, which, me, *refs):
    weights, held, refs = refs[0], refs[1], refs[2:]
    pieces, refs = refs[: len(which)], refs[len(which) :]
    parts = refs[: len(steps)]
    whole = held
    if which:
        whole, far_whole, sem = refs[len(steps) :]
        assemble_kernel(which, me, *pieces, whole)
        copy = pltpu.make_async_copy(whole, far_whole, sem)
        copy.start()
    lhs = []
    for s in steps:
        at = (place(me, first=True) + s) % N_RING
        for k in range(N_RING):
            w = weights[group(me, at, k)]
            lhs.append(jnp.concatenate([w[b] for b in range(3)], axis=1))
    res = dot(jnp.concatenate(lhs, axis=0), whole[...]).astype(BF16)
    res = res.reshape(len(steps), *parts[0].shape)
    for i, part in enumerate(parts):
        part[...] = res[i]
    if which:
        copy.wait()


def value_part(me, weights, whole, steps, pieces=(), which=()):
    _, _, rows, width = weights.shape
    n = whole.shape[1]
    shapes = [like(N_RING, rows, n)] * len(steps)
    specs = [ON_CHIP] * len(steps)
    if which:
        shapes += [like(*whole.shape), pltpu.HBM(whole.shape, BF16)]
        specs += [ON_CHIP, FAR]
    return pl.pallas_call(
        functools.partial(value_kernel, steps, which),
        out_shape=shapes,
        in_specs=[SCALAR] + [ON_CHIP] * (len(which) + 2),
        out_specs=specs,
        scratch_shapes=[pltpu.SemaphoreType.DMA] if which else [],
        input_output_aliases={2: len(steps)} if which else {},
        compiler_params=vmem(16),
        cost_estimate=pl.CostEstimate(
            flops=24 * len(steps) * rows * width * n, bytes_accessed=2 * MIB, transcendentals=0
        ),
        name="value_part",
    )(me, weights, whole, *pieces)


def weight_kernel(steps, me, whole, *refs):
    feats, (out, res, sems) = refs[: len(steps)], refs[-3:]
    _, rows, n = feats[0].shape
    width = out.shape[-1]
    copies = []
    for i, s in enumerate(steps):
        at = (place(me, first=True) + N_RING - s) % N_RING
        tall = dot_t(feats[i][...].reshape(N_RING * rows, n), whole[...]).astype(BF16)
        for k in range(N_RING):
            for b in range(3):
                res[i, k, b] = tall[k * rows : (k + 1) * rows, b * width : (b + 1) * width]
            copies.append(pltpu.make_async_copy(res.at[i, k], out.at[group(me, at, k)], sems.at[i, k]))
            copies[-1].start()
    for copy in copies:
        copy.wait()


def weight_grad(me, whole, feats, steps, begun=None):
    _, rows, n = feats[0].shape
    width = whole.shape[0] // 3
    n_steps = len(steps)
    more = [] if begun is None else [begun]
    return pl.pallas_call(
        functools.partial(weight_kernel, steps),
        out_shape=pltpu.HBM((N_RING * N_RING, 3, rows, width), BF16),
        in_specs=[SCALAR] + [ON_CHIP] * (n_steps + 1) + [FAR] * len(more),
        out_specs=FAR,
        scratch_shapes=[
            pltpu.VMEM((n_steps, N_RING, 3, rows, width), BF16),
            pltpu.SemaphoreType.DMA((n_steps, N_RING)),
        ],
        input_output_aliases={n_steps + 2: 0} if more else {},
        compiler_params=vmem(18),
        cost_estimate=pl.CostEstimate(
            flops=24 * n_steps * rows * width * n, bytes_accessed=2 * MIB, transcendentals=0
        ),
        name="weight_grad",
    )(me, whole, *feats, *more)


def first_sum_kernel(me, *refs):
    parts, outs = refs[:N_RING], refs[N_RING:]
    for s in range(N_RING):
        k = pl.ds((place(me, first=False) + s) % N_RING, 1)
        total = parts[0][k].astype(F32)
        for i in range(1, N_RING):
            total = total + parts[i][k].astype(F32)
        outs[s][...] = total[0].astype(BF16)


def first_sum(me, parts):
    _, rows, n = parts[0].shape
    return pl.pallas_call(
        first_sum_kernel,
        out_shape=[like(rows, n)] * N_RING,
        in_specs=[SCALAR] + [ON_CHIP] * N_RING,
        out_specs=[ON_CHIP] * N_RING,
        compiler_params=vmem(6),
        name="first_sum",
    )(me, *parts)


def sum_kernel(me, *refs):
    parts, outs, whole = refs[:N_RING], refs[N_RING:-1], refs[-1]
    total = parts[0][...].astype(F32)
    for i in range(1, N_RING):
        total = total + parts[i][...].astype(F32)
    whole[...] = total.astype(BF16)
    tokens = outs[0].shape[-1]
    for ahead in range(N_X):
        for other in range(2):
            outs[ahead][other] = whole[:, part_of(target(me[0], ahead, other), tokens)]


def sum_parts(me, parts):
    rows, n = parts[0].shape
    return pl.pallas_call(
        sum_kernel,
        out_shape=[like(2, rows, n // N_CTX)] * N_X,
        in_specs=[SCALAR] + [ON_CHIP] * N_RING,
        out_specs=[ON_CHIP] * N_X,
        scratch_shapes=[pltpu.VMEM((rows, n), BF16)],
        compiler_params=vmem(6),
        name="sum_parts",
    )(me, *parts)


def finish_kernel(me, *refs):
    pieces, out, whole = refs[:N_CTX], refs[N_CTX], refs[N_CTX + 1]
    sub = pieces[0].shape[0]
    for p in range(N_CTX):
        whole[part_of(source(me[0], p), sub), :] = pieces[p][...]
    out[...] = whole[...].T


def finish(me, pieces):
    rows, tokens = pieces[0].shape
    return pl.pallas_call(
        finish_kernel,
        out_shape=like(tokens, rows * N_CTX),
        in_specs=[SCALAR] + [ON_CHIP] * N_CTX,
        scratch_shapes=[pltpu.VMEM((rows * N_CTX, tokens), BF16)],
        compiler_params=vmem(6),
        name="finish",
    )(me, *pieces)


def tie(a, b):
    return lax.optimization_barrier((a, b))


def per_device(features_in, w_featurizer, filter_taps, query_proj, key_proj, value_proj, grad_mixed):
    width_dev = features_in.shape[1]
    me = jnp.stack([lax.axis_index("ctx"), lax.axis_index("tp")]).astype(jnp.int32)
    weights = w_featurizer.transpose(0, 2, 1, 3)
    ready = prepare(me, (key_proj, value_proj, grad_mixed, query_proj, features_in))
    along = [ready[0]] + [shift_x(ready[s], s) for s in (1, 2, 3)]
    spec_taps = taps_spectrum(filter_taps.reshape(width_dev // N_CTX, -1))
    along, spec_taps = tie(along, spec_taps)
    *table, hr, hi, hn = spec_taps
    pieces = [a[0] for a in along] + [swap_core(a[1]) for a in along]
    grads, grad_taps = convolutions(me, pieces, table, (hr, hi, hn))
    own, sibling, next1, next2 = gather_start(grads)
    sibling, pieces = tie(sibling, pieces)
    feats = join_features(me, pieces)
    feats = [feats] + [shift_ring(feats, s, first=False) for s in (1, 2, 3)]
    next1, feats[1] = tie(next1, feats[1])
    last = spin(next1)
    last, feats = tie(last, feats)
    pieces = (own, sibling, next1, next2, swap_core(next1), swap_core(next2))
    whole = assemble(me, pieces, (0, 1, 2, 3, 5, 6))
    *sent, whole, far_whole = value_part(me, weights, whole, (1, 2, 3), (last, swap_core(last)), (4, 7))
    parts = [shift_ring(p, s, first=True) for p, s in zip(sent, (1, 2, 3), strict=True)]
    feats = stack(me, feats)
    feats1, feats3 = shift_ring(feats, 1, first=True), shift_ring(feats, 3, first=True)
    (part,) = value_part(me, weights, whole, (0,))
    part, feats = tie(part, feats)
    parts = [part, *parts]
    parts = first_sum(me, parts)
    parts, (feats1, feats3) = tie(parts, (feats1, feats3))
    parts = [parts[0]] + [shift_ring(parts[s], s, first=False) for s in (1, 2, 3)]
    feats = [feats, feats1, shift_ring(feats, 2, first=True), feats3]
    grad_w = weight_grad(me, far_whole, [feats[s] for s in (0, 1, 3)], (0, 1, 3))
    parts, grad_w = tie(parts, grad_w)
    ready = sum_parts(me, parts)
    along = [ready[0]] + [shift_x(ready[s], s) for s in (1, 2, 3)]
    grad_w = weight_grad(me, far_whole, [feats[2]], (2,), grad_w)
    along, grad_w = tie(along, grad_w)
    grad_features = finish(me, [a[0] for a in along] + [swap_core(a[1]) for a in along])
    return grad_features, grad_w.transpose(0, 2, 1, 3), grad_taps.reshape(filter_taps.shape)


def solution(mesh):
    return jax.shard_map(
        per_device,
        mesh=mesh,
        in_specs=(
            P("ctx", "tp"),
            P(None, "ctx", None, "tp"),
            P("tp", "ctx", None),
            P("ctx", "tp"),
            P("ctx", "tp"),
            P("ctx", "tp"),
            P("ctx", "tp"),
        ),
        out_specs=(P("ctx", "tp"), P(None, "ctx", None, "tp"), P("tp", "ctx", None)),
        check_vma=False,
    )
```

```python
import functools
import math

import jax
import jax.numpy as jnp
import numpy as np
from jax import lax
from jax.experimental import pallas as pl
from jax.experimental.pallas import tpu as pltpu
from jax.sharding import PartitionSpec as P

BF16 = jnp.bfloat16
F32 = jnp.float32
N_X = 4
N_CTX = 8
N_RING = 4
MIB = 1024 * 1024
ON_CHIP = pl.BlockSpec(memory_space=pltpu.VMEM)
FAR = pl.BlockSpec(memory_space=pltpu.HBM)
SCALAR = pl.BlockSpec(memory_space=pltpu.SMEM)


def vmem(mib):
    return pltpu.CompilerParams(vmem_limit_bytes=mib * MIB)


def like(*shape, dtype=BF16):
    return jax.ShapeDtypeStruct(shape, dtype)


def tables(n):
    idx = np.arange(n, dtype=np.int64)
    angle = (np.outer(idx, idx) % (2 * n)).astype(np.float64) * (math.pi / n)
    return [jnp.asarray(whole.astype(BF16)) for whole in (np.cos(angle), np.sin(angle))]


def dot(a, b):
    return lax.dot_general(a, b, (((1,), (0,)), ((), ())), preferred_element_type=F32)


def dot_t(a, b):
    return lax.dot_general(a, b, (((1,), (1,)), ((), ())), preferred_element_type=F32)


def shift_x(a, steps):
    return lax.ppermute(a, "ctx", [(i, (i + 2 * steps) % N_CTX) for i in range(N_CTX)])


def swap_core(a):
    return lax.ppermute(a, "ctx", [(i, i ^ 1) for i in range(N_CTX)])


def source(me, piece):
    back, other = piece % N_X, piece // N_X
    chip = (me // 2 + N_X - back) % N_X
    core = me % 2
    return 2 * chip + (1 - core if other else core)


def spin(a):
    pairs = [(2 * x + core, 2 * ((x + 1 - 2 * core) % N_X) + core) for x in range(N_X) for core in range(2)]
    return lax.ppermute(a, "ctx", pairs)


def gather_start(mine):
    sibling = swap_core(mine)
    return [mine, sibling, spin(mine), spin(sibling)]


def gathered_source(me, piece):
    chip, core = me // 2, me % 2
    if piece < 2:
        return 2 * chip + (core if piece == 0 else 1 - core)
    kind, theirs = (piece - 2) % 3, piece >= 5
    back = 1 - 2 * core
    if theirs:
        back, core = -back, 1 - core
    chip = (chip + N_X - (2 if kind == 2 else back)) % N_X
    return 2 * chip + (1 - core if kind == 1 else core)


def target(me, ahead, other):
    chip = (me // 2 + ahead) % N_X
    core = me % 2
    return 2 * chip + (1 - core if other else core)


def place(me, first):
    on_y, on_z = me[1] // N_RING, me[1] % N_RING
    return jnp.where((me[0] % 2 == 0) == first, on_y, on_z)


def group(me, at, k):
    return jnp.where(me[0] % 2 == 0, at * N_RING + k, k * N_RING + at)


def shift_ring(a, steps, first):
    pairs = []
    for ctx in range(N_CTX):
        for y in range(N_RING):
            for z in range(N_RING):
                along_y = (ctx % 2 == 0) == first
                to = ((y + steps) % N_RING, z) if along_y else (y, (z + steps) % N_RING)
                base = ctx * N_RING * N_RING
                pairs.append((base + y * N_RING + z, base + to[0] * N_RING + to[1]))
    return lax.ppermute(a, ("ctx", "tp"), pairs)


def part_of(index, size):
    return pl.ds(pl.multiple_of(index * size, size), size)


def prep_kernel(me, *refs):
    n_arr = len(refs) - 3 - N_X
    arrays, outs = refs[:n_arr], refs[n_arr : n_arr + N_X]
    local, turned, sems = refs[n_arr + N_X :]
    copies = [pltpu.make_async_copy(arrays[a], local.at[a], sems.at[a]) for a in range(n_arr)]
    for copy in copies:
        copy.start()
    sub = outs[0].shape[2]
    for a in range(n_arr):
        copies[a].wait()
        turned[a] = local[a].T
    for ahead in range(N_X):
        for other in range(2):
            rows = part_of(target(me[0], ahead, other), sub)
            for a in range(n_arr):
                outs[ahead][other, a] = turned[a, rows, :]


def prepare(me, arrays):
    tokens, width = arrays[0].shape
    n_arr = len(arrays)
    return pl.pallas_call(
        prep_kernel,
        out_shape=[like(2, n_arr, width // N_CTX, tokens)] * N_X,
        in_specs=[SCALAR] + [FAR] * n_arr,
        out_specs=[ON_CHIP] * N_X,
        scratch_shapes=[
            pltpu.VMEM((n_arr, tokens, width), BF16),
            pltpu.VMEM((n_arr, width, tokens), BF16),
            pltpu.SemaphoreType.DMA((n_arr,)),
        ],
        compiler_params=vmem(6),
        name="prepare",
    )(me, *[pltpu.with_memory_space_constraint(a, pltpu.HBM) for a in arrays])


def join_kernel(me, *refs):
    pieces, out = refs[:N_CTX], refs[N_CTX]
    span = pieces[0].shape[-1]
    for p in range(N_CTX):
        out[:, part_of(source(me[0], p), span)] = pieces[p][pieces[p].shape[0] - 1]


def join_features(me, pieces):
    _, sub, span = pieces[0].shape
    return pl.pallas_call(
        join_kernel,
        out_shape=like(sub, span * N_CTX),
        in_specs=[SCALAR] + [ON_CHIP] * N_CTX,
        out_specs=ON_CHIP,
        compiler_params=vmem(6),
        name="join_features",
    )(me, *pieces)


def stack_kernel(me, *refs):
    pieces, out = refs[:N_RING], refs[N_RING]
    for s in range(N_RING):
        out[pl.ds((place(me, first=False) + N_RING - s) % N_RING, 1)] = pieces[s][...][None]


def stack(me, pieces):
    return pl.pallas_call(
        stack_kernel,
        out_shape=like(N_RING, *pieces[0].shape),
        in_specs=[SCALAR] + [ON_CHIP] * N_RING,
        out_specs=ON_CHIP,
        compiler_params=vmem(6),
        name="stack_features",
    )(me, *pieces)


def signs(n):
    lane = lax.broadcasted_iota(jnp.int32, (1, n), 1)
    return jnp.where(lane % 2 == 0, 1.0, -1.0).astype(F32)


def spectrum(signals, table, n):
    nyq = jnp.sum(signals.astype(F32) * signs(n), axis=1, keepdims=True)
    return dot(signals, table[0][...]), dot(signals, table[1][...]), nyq


def split(a):
    high = a.astype(BF16)
    return high, (a - high.astype(F32)).astype(BF16)


def inverse(re, im, nyq, table, n):
    rows = re.shape[0]
    lane = lax.broadcasted_iota(jnp.int32, (1, n), 1)
    weight = jnp.where(lane == 0, 0.5 / n, 1.0 / n).astype(F32)
    re_hi, re_lo = split(re * weight)
    im_hi, im_lo = split(im * weight)
    both = dot(jnp.concatenate([re_hi, re_lo], axis=0), table[0][...])
    both = both + dot(jnp.concatenate([im_hi, im_lo], axis=0), table[1][...])
    return both[:rows] + both[rows:] + (nyq * (0.5 / n)) * signs(n)


def taps_kernel(*refs):
    far, taps = refs[:2], refs[2]
    table, (re, im, nyq, sems) = refs[3:5], refs[5:]
    copies = [pltpu.make_async_copy(far[i], table[i], sems.at[i]) for i in range(2)]
    for copy in copies:
        copy.start()
    for copy in copies:
        copy.wait()
    re[...], im[...], nyq[...] = spectrum(taps[...], table, taps.shape[1])


def taps_spectrum(taps):
    chans, n = taps.shape
    return pl.pallas_call(
        taps_kernel,
        out_shape=[like(n, n)] * 2 + [like(chans, n, dtype=F32)] * 2 + [like(chans, 1, dtype=F32)],
        in_specs=[FAR] * 2 + [ON_CHIP],
        out_specs=[ON_CHIP] * 5,
        scratch_shapes=[pltpu.SemaphoreType.DMA((2,))],
        compiler_params=vmem(12),
        cost_estimate=pl.CostEstimate(flops=8 * chans * n * n, bytes_accessed=8 * MIB, transcendentals=0),
        name="taps_spectrum",
    )(*[pltpu.with_memory_space_constraint(t, pltpu.HBM) for t in tables(n)], taps)


def conv_kernel(me, *refs):
    pieces = refs[:N_CTX]
    table = refs[N_CTX : N_CTX + 2]
    hr, hi, hn = refs[N_CTX + 2 : N_CTX + 5]
    grads, grad_taps, whole = refs[N_CTX + 5 :]
    chans, span = pieces[0].shape[-2:]
    n = N_CTX * span
    for p in range(N_CTX):
        for a in range(4):
            whole[a, :, part_of(source(me[0], p), span)] = pieces[p][a]
    product = (whole[0].astype(F32) * whole[1].astype(F32)).astype(BF16)
    grad_conv = (whole[2].astype(F32) * whole[3].astype(F32)).astype(BF16)
    re, im, nyq = spectrum(jnp.concatenate([product, grad_conv], axis=0), table, n)
    ur, gr, ui, gi, un, gn = re[:chans], re[chans:], im[:chans], im[chans:], nyq[:chans], nyq[chans:]
    hr, hi, hn = hr[...], hi[...], hn[...]
    spec_re = jnp.concatenate([ur * hr - ui * hi, gr * hr + gi * hi, gr * ur + gi * ui], axis=0)
    spec_im = jnp.concatenate([ur * hi + ui * hr, gi * hr - gr * hi, gi * ur - gr * ui], axis=0)
    out = inverse(spec_re, spec_im, jnp.concatenate([un * hn, gn * hn, gn * un], axis=0), table, n)
    out, grad_taps[...] = out[: 2 * chans], out[2 * chans :].astype(BF16)
    grads[0] = (whole[2].astype(F32) * out[:chans]).astype(BF16)
    grads[1] = (out[chans:] * whole[1].astype(F32)).astype(BF16)
    grads[2] = (out[chans:] * whole[0].astype(F32)).astype(BF16)


def convolutions(me, pieces, table, taps_spec):
    chans, span = pieces[0].shape[-2:]
    n = N_CTX * span
    return pl.pallas_call(
        conv_kernel,
        out_shape=[like(3, chans, n), like(chans, n)],
        in_specs=[SCALAR] + [ON_CHIP] * (N_CTX + 5),
        out_specs=[ON_CHIP] * 2,
        scratch_shapes=[pltpu.VMEM((4, chans, n), BF16)],
        compiler_params=vmem(20),
        cost_estimate=pl.CostEstimate(flops=32 * chans * n * n, bytes_accessed=8 * MIB, transcendentals=0),
        name="convolutions",
    )(me, *pieces, *table, *taps_spec)


def gather_pieces(mine):
    along = [mine] + [shift_x(mine, s) for s in (1, 2, 3)]
    return along + [swap_core(a) for a in along]


def assemble_kernel(which, me, *refs):
    pieces, whole = refs[: len(which)], refs[-1]
    sub = pieces[0].shape[1]
    for p, piece in zip(which, pieces, strict=True):
        for b in range(3):
            whole[part_of(b * N_CTX + gathered_source(me[0], p), sub), :] = piece[b]


def assemble(me, pieces, which):
    _, sub, n = pieces[0].shape
    return pl.pallas_call(
        functools.partial(assemble_kernel, which),
        out_shape=like(3 * N_CTX * sub, n),
        in_specs=[SCALAR] + [ON_CHIP] * len(which),
        out_specs=ON_CHIP,
        compiler_params=vmem(8),
        name="assemble",
    )(me, *pieces)


def value_kernel(steps, which, me, *refs):
    weights, held, refs = refs[0], refs[1], refs[2:]
    pieces, refs = refs[: len(which)], refs[len(which) :]
    parts = refs[: len(steps)]
    whole = held
    if which:
        whole, far_whole, sem = refs[len(steps) :]
        assemble_kernel(which, me, *pieces, whole)
        copy = pltpu.make_async_copy(whole, far_whole, sem)
        copy.start()
    lhs = []
    for s in steps:
        at = (place(me, first=True) + s) % N_RING
        for k in range(N_RING):
            w = weights[group(me, at, k)]
            lhs.append(jnp.concatenate([w[b] for b in range(3)], axis=1))
    res = dot(jnp.concatenate(lhs, axis=0), whole[...]).astype(BF16)
    res = res.reshape(len(steps), *parts[0].shape)
    for i, part in enumerate(parts):
        part[...] = res[i]
    if which:
        copy.wait()


def value_part(me, weights, whole, steps, pieces=(), which=()):
    _, _, rows, width = weights.shape
    n = whole.shape[1]
    shapes = [like(N_RING, rows, n)] * len(steps)
    specs = [ON_CHIP] * len(steps)
    if which:
        shapes += [like(*whole.shape), pltpu.HBM(whole.shape, BF16)]
        specs += [ON_CHIP, FAR]
    return pl.pallas_call(
        functools.partial(value_kernel, steps, which),
        out_shape=shapes,
        in_specs=[SCALAR] + [ON_CHIP] * (len(which) + 2),
        out_specs=specs,
        scratch_shapes=[pltpu.SemaphoreType.DMA] if which else [],
        input_output_aliases={2: len(steps)} if which else {},
        compiler_params=vmem(16),
        cost_estimate=pl.CostEstimate(
            flops=24 * len(steps) * rows * width * n, bytes_accessed=2 * MIB, transcendentals=0
        ),
        name="value_part",
    )(me, weights, whole, *pieces)


def weight_kernel(steps, me, whole, *refs):
    feats, (out, res, sems) = refs[: len(steps)], refs[-3:]
    _, rows, n = feats[0].shape
    width = out.shape[-1]
    copies = []
    for i, s in enumerate(steps):
        at = (place(me, first=True) + N_RING - s) % N_RING
        tall = dot_t(feats[i][...].reshape(N_RING * rows, n), whole[...]).astype(BF16)
        for k in range(N_RING):
            for b in range(3):
                res[i, k, b] = tall[k * rows : (k + 1) * rows, b * width : (b + 1) * width]
            copies.append(pltpu.make_async_copy(res.at[i, k], out.at[group(me, at, k)], sems.at[i, k]))
            copies[-1].start()
    for copy in copies:
        copy.wait()


def weight_grad(me, whole, feats, steps, begun=None):
    _, rows, n = feats[0].shape
    width = whole.shape[0] // 3
    n_steps = len(steps)
    more = [] if begun is None else [begun]
    return pl.pallas_call(
        functools.partial(weight_kernel, steps),
        out_shape=pltpu.HBM((N_RING * N_RING, 3, rows, width), BF16),
        in_specs=[SCALAR] + [ON_CHIP] * (n_steps + 1) + [FAR] * len(more),
        out_specs=FAR,
        scratch_shapes=[
            pltpu.VMEM((n_steps, N_RING, 3, rows, width), BF16),
            pltpu.SemaphoreType.DMA((n_steps, N_RING)),
        ],
        input_output_aliases={n_steps + 2: 0} if more else {},
        compiler_params=vmem(18),
        cost_estimate=pl.CostEstimate(
            flops=24 * n_steps * rows * width * n, bytes_accessed=2 * MIB, transcendentals=0
        ),
        name="weight_grad",
    )(me, whole, *feats, *more)


def first_sum_kernel(me, *refs):
    parts, outs = refs[:N_RING], refs[N_RING:]
    for s in range(N_RING):
        k = pl.ds((place(me, first=False) + s) % N_RING, 1)
        total = parts[0][k].astype(F32)
        for i in range(1, N_RING):
            total = total + parts[i][k].astype(F32)
        outs[s][...] = total[0].astype(BF16)


def first_sum(me, parts):
    _, rows, n = parts[0].shape
    return pl.pallas_call(
        first_sum_kernel,
        out_shape=[like(rows, n)] * N_RING,
        in_specs=[SCALAR] + [ON_CHIP] * N_RING,
        out_specs=[ON_CHIP] * N_RING,
        compiler_params=vmem(6),
        name="first_sum",
    )(me, *parts)


def sum_kernel(*refs):
    parts, out = refs[:N_RING], refs[N_RING]
    total = parts[0][...].astype(F32)
    for i in range(1, N_RING):
        total = total + parts[i][...].astype(F32)
    tokens = out.shape[-1]
    for i in range(N_CTX):
        out[i] = total[:, i * tokens : (i + 1) * tokens].astype(BF16)


def sum_parts(parts):
    rows, n = parts[0].shape
    return pl.pallas_call(
        sum_kernel,
        out_shape=like(N_CTX, rows, n // N_CTX),
        in_specs=[ON_CHIP] * N_RING,
        out_specs=ON_CHIP,
        compiler_params=vmem(6),
        name="sum_parts",
    )(*parts)


def finish_kernel(pieces, out):
    n_ctx, sub, tokens = pieces.shape
    out[...] = pieces[...].reshape(n_ctx * sub, tokens).T


def finish(pieces):
    n_ctx, sub, tokens = pieces.shape
    return pl.pallas_call(
        finish_kernel,
        out_shape=like(tokens, n_ctx * sub),
        in_specs=[ON_CHIP],
        compiler_params=vmem(6),
        name="finish",
    )(pieces)


def tie(a, b):
    return lax.optimization_barrier((a, b))


def per_device(features_in, w_featurizer, filter_taps, query_proj, key_proj, value_proj, grad_mixed):
    width_dev = features_in.shape[1]
    me = jnp.stack([lax.axis_index("ctx"), lax.axis_index("tp")]).astype(jnp.int32)
    weights = w_featurizer.transpose(0, 2, 1, 3)
    ready = prepare(me, (key_proj, value_proj, grad_mixed, query_proj, features_in))
    along = [ready[0]] + [shift_x(ready[s], s) for s in (1, 2, 3)]
    spec_taps = taps_spectrum(filter_taps.reshape(width_dev // N_CTX, -1))
    along, spec_taps = tie(along, spec_taps)
    *table, hr, hi, hn = spec_taps
    pieces = [a[0] for a in along] + [swap_core(a[1]) for a in along]
    grads, grad_taps = convolutions(me, pieces, table, (hr, hi, hn))
    own, sibling, next1, next2 = gather_start(grads)
    sibling, pieces = tie(sibling, pieces)
    feats = join_features(me, pieces)
    feats = [feats] + [shift_ring(feats, s, first=False) for s in (1, 2, 3)]
    next1, feats[1] = tie(next1, feats[1])
    last = spin(next1)
    last, feats = tie(last, feats)
    pieces = (own, sibling, next1, next2, swap_core(next1), swap_core(next2))
    whole = assemble(me, pieces, (0, 1, 2, 3, 5, 6))
    *sent, whole, far_whole = value_part(me, weights, whole, (1, 2, 3), (last, swap_core(last)), (4, 7))
    parts = [shift_ring(p, s, first=True) for p, s in zip(sent, (1, 2, 3), strict=True)]
    feats = stack(me, feats)
    feats1, feats3 = shift_ring(feats, 1, first=True), shift_ring(feats, 3, first=True)
    (part,) = value_part(me, weights, whole, (0,))
    part, feats = tie(part, feats)
    parts = [part, *parts]
    parts = first_sum(me, parts)
    parts, (feats1, feats3) = tie(parts, (feats1, feats3))
    parts = [parts[0]] + [shift_ring(parts[s], s, first=False) for s in (1, 2, 3)]
    feats = [feats, feats1, shift_ring(feats, 2, first=True), feats3]
    grad_w = weight_grad(me, far_whole, [feats[s] for s in (0, 1, 3)], (0, 1, 3))
    parts, grad_w = tie(parts, grad_w)
    moved = lax.all_to_all(sum_parts(parts), "ctx", 0, 0)
    grad_w = weight_grad(me, far_whole, [feats[2]], (2,), grad_w)
    moved, grad_w = tie(moved, grad_w)
    grad_features = finish(moved)
    return grad_features, grad_w.transpose(0, 2, 1, 3), grad_taps.reshape(filter_taps.shape)


def solution(mesh):
    return jax.shard_map(
        per_device,
        mesh=mesh,
        in_specs=(
            P("ctx", "tp"),
            P(None, "ctx", None, "tp"),
            P("tp", "ctx", None),
            P("ctx", "tp"),
            P("ctx", "tp"),
            P("ctx", "tp"),
            P("ctx", "tp"),
        ),
        out_specs=(P("ctx", "tp"), P(None, "ctx", None, "tp"), P("tp", "ctx", None)),
        check_vma=False,
    )
```
